512 devices in a mesh: row: 16 (over y, x), col: 32 (over z, core).
Axes of the slice: x: 4, y: 4, z: 16, core: 2. Of those that a mesh axis runs over, the one named last changes fastest.
Arguments:
- matrix: float32 [8192, 8192], P('row', 'col'), may hold values from -6 to 6
- row_struct: int32 [2, 32], P(None, 'row'), may hold values from 0 to 1
- col_struct: int32 [2, 32], P(None, 'col'), may hold values from 0 to 1
- panel_index: int32 [2], replicated, may hold values from 0 to 30, as said below
- lower_inv: float32 [2, 512, 512], replicated, as said below
- upper_inv: float32 [2, 512, 512], replicated, as said below
Outputs:
- factored: float32 [8192, 8192], P('row', 'col')
The draws below stay inside these ranges and needn't reach their ends.
Inputs may be any that keep to these rules, and one draw needn't show every extreme that they name: `panel_index`: even block indices; the two steps' panels are disjoint; one of them is the last block pair. `lower_inv`: unit lower triangular. `upper_inv`: upper triangular with positive diagonal.
All inputs are finite; a program needn't handle non-finite values.
Results may differ from the reference program's by a relative error of at most 0.0001.
Values sent between devices are 32-bit elements; how exact they have to be, the bound alone decides.
No kernel may reach another device: no remote copies, remote signals or barrier semaphores. Data moves between devices by JAX's collectives and lax.ppermute only.
A program may use at most 64 MiB of HBM per device.

```python
import jax
import jax.numpy as jnp
from jax import lax

NB = 256
PW = 512
LC = 1
STEPS = 2
LR = 2
NBLK = 32
N = 8192
N_ROW = 16
N_COL = 32


def panel_layout(key):
    halves = NBLK // 2
    other_half = jax.random.randint(jax.random.fold_in(key, 11), (), 0, halves - 1)
    order_bit = jax.random.randint(jax.random.fold_in(key, 12), (), 0, 2)
    last_half = jnp.int32(halves - 1)
    first_half = jnp.where(order_bit > 0, last_half, other_half)
    second_half = jnp.where(order_bit > 0, other_half, last_half)
    return jnp.stack([2 * first_half, 2 * second_half]).astype(jnp.int32)


def structure_mask(key, salt, block_ids):
    panels = panel_layout(key)
    random_bits = jax.random.randint(jax.random.fold_in(key, salt), (2, NBLK), 0, 2).astype(jnp.int32)
    in_first = (block_ids >= panels[0]) & (block_ids < panels[0] + 2)
    in_second = (block_ids >= panels[1]) & (block_ids < panels[1] + 2)
    step_zero = jnp.where(in_first, 0, jnp.where(in_second, 1, random_bits[0]))
    step_one = jnp.where(in_first | in_second, 0, random_bits[1])
    return jnp.stack([step_zero, step_one]).astype(jnp.int32)


def draw_panel_index(key, part):
    return panel_layout(key)


def draw_row_struct(key, part):
    places = jnp.arange(NBLK, dtype=jnp.int32)
    block_ids = places % LR * N_ROW + places // LR
    return structure_mask(key, 21, block_ids)


def draw_col_struct(key, part):
    places = jnp.arange(NBLK, dtype=jnp.int32)
    block_ids = places % LC * N_COL + places // LC
    return structure_mask(key, 31, block_ids)


def unit_noise(key, shape):
    return jax.random.normal(key, shape, jnp.float32)


def draw_lower_inv(key, part):
    noise = unit_noise(jax.random.fold_in(key, 41), (STEPS, PW, PW))
    lower = jnp.tril(noise * (0.6 / PW ** 0.5), -1)
    return lower + jnp.eye(PW, dtype=jnp.float32)[None, :, :]


def draw_upper_inv(key, part):
    noise = unit_noise(jax.random.fold_in(key, 51), (STEPS, PW, PW))
    upper = jnp.triu(noise * (0.6 / PW), 1)
    spread = jax.random.uniform(jax.random.fold_in(key, 52), (STEPS, PW), jnp.float32, -0.6931472, 0.6931472)
    diagonal = jnp.exp(spread) / PW ** 0.5
    return upper + diagonal[:, :, None] * jnp.eye(PW, dtype=jnp.float32)[None, :, :]


def block_levels(own_key, shape, cuts, least, top_value):
    level, own = 1.0, jax.random.fold_in(own_key, 6)
    for position, shards_of in cuts:
        draws = jnp.exp(jax.random.uniform(jax.random.fold_in(own, position), (shards_of,), jnp.float32, least / len(cuts), top_value / len(cuts)))
        level = level * jnp.repeat(draws, shape[position] // shards_of).reshape([-1 if axis == position else 1 for axis in range(len(shape))])
    return level


def bell_draw(rng, shape, width, bound, split=(), kind=jnp.bfloat16):
    values = jax.random.normal(rng, shape, jnp.float32) * width
    if len(split) > 0:
        values = block_levels(rng, shape, split, -0.22, 0.18) * values
    return jnp.clip(values, min=-bound, max=bound).astype(kind)


def setup_inputs(seed: int = 0) -> dict:
    seeds = jax.random.split(jax.random.key(seed), 7)
    matrix = bell_draw(seeds[0], (N, N), 1.0, 6.0, ((0, 16), (1, 32)), jnp.float32)
    row_struct = draw_row_struct(jax.random.fold_in(seeds[6], 71), 0)
    col_struct = draw_col_struct(jax.random.fold_in(seeds[6], 71), 0)
    panel_index = draw_panel_index(jax.random.fold_in(seeds[6], 71), 0)
    lower_inv = draw_lower_inv(jax.random.fold_in(seeds[6], 71), 0)
    upper_inv = draw_upper_inv(jax.random.fold_in(seeds[6], 71), 0)
    return {"matrix": matrix, "row_struct": row_struct, "col_struct": col_struct, "panel_index": panel_index, "lower_inv": lower_inv, "upper_inv": upper_inv}


def to_global(stored):
    shaped = stored.reshape(N_ROW, LR, NB, N_COL, LC, NB)
    return shaped.transpose(1, 0, 2, 4, 3, 5).reshape(N, N)


def to_storage(dense):
    shaped = dense.reshape(LR, N_ROW, NB, LC, N_COL, NB)
    return shaped.transpose(1, 0, 2, 4, 3, 5).reshape(N, N)


def reference(matrix, row_struct, col_struct, panel_index, lower_inv, upper_inv):
    dense = to_global(matrix)
    rows_global = row_struct.reshape(STEPS, N_ROW, LR).transpose(0, 2, 1).reshape(STEPS, NBLK)
    cols_global = col_struct.reshape(STEPS, N_COL, LC).transpose(0, 2, 1).reshape(STEPS, NBLK)
    highest = lax.Precision.HIGHEST
    for panel_step in range(STEPS):
        offset = (panel_index[panel_step] * NB).astype(jnp.int32)
        panel_cols = lax.dynamic_slice_in_dim(dense, offset, PW, 1)
        panel_rows = lax.dynamic_slice_in_dim(dense, offset, PW, 0)
        lower_part = jnp.dot(panel_cols, upper_inv[panel_step], precision=highest, preferred_element_type=jnp.float32)
        upper_part = jnp.dot(lower_inv[panel_step], panel_rows, precision=highest, preferred_element_type=jnp.float32)
        row_keep = jnp.repeat(rows_global[panel_step], NB) > 0
        col_keep = jnp.repeat(cols_global[panel_step], NB) > 0
        lower_masked = jnp.where(row_keep[:, None], lower_part, jnp.float32(0.0))
        upper_masked = jnp.where(col_keep[None, :], upper_part, jnp.float32(0.0))
        dense = dense - jnp.dot(lower_masked, upper_masked, precision=highest, preferred_element_type=jnp.float32)
        new_cols = jnp.where(row_keep[:, None], lower_part, lax.dynamic_slice_in_dim(dense, offset, PW, 1))
        dense = lax.dynamic_update_slice_in_dim(dense, new_cols, offset, 1)
        new_rows = jnp.where(col_keep[None, :], upper_part, lax.dynamic_slice_in_dim(dense, offset, PW, 0))
        dense = lax.dynamic_update_slice_in_dim(dense, new_rows, offset, 0)
    return to_storage(dense)
```

```python
import jax
import jax.numpy as jnp
from jax import lax
from jax.sharding import PartitionSpec as P

PREC = lax.Precision.HIGH


def dot(a, b):
    return jnp.dot(a, b, precision=PREC, preferred_element_type=jnp.float32)


def make_fetch(plane, n_z, n_x, n_y):
    first = 2 * plane
    n_row = n_x * n_y
    row_root = first % n_row
    slot = first // n_row
    y0, x0 = row_root // n_x, row_root % n_x

    def send_z(value, hops):
        pairs = [
            (2 * (a % n_z) + core, 2 * (b % n_z) + core) for a, b in hops for core in range(2)
        ]
        return lax.ppermute(value, "col", pairs)

    def send_xy(value, hops):
        pairs = [
            ((ya % n_y) * n_x + xa % n_x, (yb % n_y) * n_x + xb % n_x)
            for (ya, xa), (yb, xb) in hops
        ]
        return lax.ppermute(value, "row", pairs)

    def fetch(block):
        size = block.shape[0] // 2
        my_z = lax.axis_index("col") // 2
        my_row = lax.axis_index("row")
        my_y, my_x = my_row // n_x, my_row % n_x
        dist = (my_z - plane) % n_z

        def among(places):
            hit = dist == places[0]
            for place in places[1:]:
                hit = hit | (dist == place)
            return hit

        far = [send_z(block, [(plane, plane + hop)]) for hop in (6, -6, 3, -3)]
        own = lax.slice_in_dim(block, slot * size, (slot + 1) * size, axis=0)
        along_y = [
            send_xy(own, [((y0, x), (y0 + hop, x)) for x in (x0, x0 + 1)]) for hop in (1, -1, 2)
        ]
        y_dist = (my_y - y0) % n_y
        piece = jnp.where(
            y_dist == 0,
            own,
            jnp.where(
                y_dist == 1, along_y[0], jnp.where(y_dist == n_y - 1, along_y[1], along_y[2])
            ),
        )
        ys = range(n_y)
        right = send_xy(
            piece,
            [((y, x0), (y, x0 + 1)) for y in ys] + [((y, x0 + 1), (y, x0 + 2)) for y in ys],
        )
        left = send_xy(
            piece,
            [((y, x0 + 1), (y, x0)) for y in ys] + [((y, x0), (y, x0 - 1)) for y in ys],
        )
        over = send_xy(
            piece,
            [((y, x0), (y, x0 + 2)) for y in ys] + [((y, x0 + 1), (y, x0 + 3)) for y in ys],
        )
        x_dist = (my_x - x0) % n_x

        def by_x(values):
            out = values[3]
            for place in (2, 1, 0):
                out = jnp.where(x_dist == place, values[place], out)
            return out

        rows = jnp.concatenate(
            [by_x([piece, right, over, left]), by_x([left, piece, right, over])], axis=0
        )
        mid = block
        for value, place in zip(far, (6, n_z - 6, 3, n_z - 3)):
            mid = jnp.where(dist == place, value, mid)
        heads = (0, 3, 6, 10, 13)
        up = send_z(mid, [(plane + h, plane + h + 1) for h in heads])
        down = send_z(mid, [(plane + h, plane + h - 1) for h in heads])
        top = send_z(mid[:size], [(plane + 6, plane + 8)])
        bottom = send_z(mid[size:], [(plane + 10, plane + 8)])
        out = jnp.where(among((1, 4, 7, 11, 14)), up, mid)
        out = jnp.where(among((15, 2, 5, 9, 12)), down, out)
        out = jnp.where(dist == 8, jnp.concatenate([top, bottom], axis=0), out)
        return out, rows

    return fetch


def local(matrix, row_struct, col_struct, panel_index, lower_inv, upper_inv):
    n_row = lax.axis_size("row")
    n_col = lax.axis_size("col")
    n_x, n_y, n_z = 4, n_row // 4, n_col // 2
    my_row = lax.axis_index("row")
    my_col = lax.axis_index("col")
    core = my_col % 2
    width = upper_inv.shape[1]
    size = width // 2
    block = matrix
    fetches = [make_fetch(plane, n_z, n_x, n_y) for plane in range(n_z)]
    for step in range(panel_index.shape[0]):
        first = panel_index[step]
        plane = first // 2
        mine, rows = lax.switch(plane, fetches, block)
        other = lax.ppermute(mine, "col", [(i, i ^ 1) for i in range(n_col)])
        upper = dot(lower_inv[step], rows)
        u_mine = lax.dynamic_slice_in_dim(upper_inv[step], core * size, size, 0)
        u_other = lax.dynamic_slice_in_dim(upper_inv[step], (1 - core) * size, size, 0)
        lower = dot(mine, u_mine) + dot(other, u_other)
        row_hit = jnp.repeat(row_struct[step] > 0, size)[:, None]
        col_hit = col_struct[step, 0] > 0
        schur = dot(
            jnp.where(row_hit, lower, jnp.float32(0.0)),
            jnp.where(col_hit, upper, jnp.float32(0.0)),
        )
        block = block - schur
        lower_mine = lax.dynamic_slice_in_dim(lower, core * size, size, 1)
        block = jnp.where((my_col // 2 == plane) & row_hit, lower_mine, block)
        for member in range(2):
            root, slot = (first + member) % n_row, (first + member) // n_row
            take = jnp.repeat(jnp.arange(2) == slot, size)[:, None] & (my_row == root) & col_hit
            part = upper[member * size : (member + 1) * size]
            block = jnp.where(take, jnp.concatenate([part, part], axis=0), block)
    return block


def solution(mesh):
    return jax.shard_map(
        local,
        mesh=mesh,
        in_specs=(P("row", "col"), P(None, "row"), P(None, "col"), P(), P(), P()),
        out_specs=P("row", "col"),
        check_vma=False,
    )
```

```python
import jax
import jax.numpy as jnp
from jax import lax
from jax.sharding import PartitionSpec as P

PREC = lax.Precision.HIGH


def dot(a, b):
    return jnp.dot(a, b, precision=PREC, preferred_element_type=jnp.float32)


def local(matrix, row_struct, col_struct, panel_index, lower_inv, upper_inv):
    n_row = lax.axis_size("row")
    n_col = lax.axis_size("col")
    n_z = n_col // 2
    my_row = lax.axis_index("row")
    my_col = lax.axis_index("col")
    my_z, core = my_col // 2, my_col % 2
    width = upper_inv.shape[1]
    size = width // 2
    def send_z(value, hops):
        pairs = [(2 * (a % n_z) + c, 2 * (b % n_z) + c) for a, b in hops for c in range(2)]
        return lax.ppermute(value, "col", pairs)

    def from_class(value, place, spacing, hop):
        return send_z(value, [(z, z + hop) for z in range(place % spacing, n_z, spacing)])

    def exchange(value):
        return lax.all_to_all(value, "row", 0, 0, tiled=True)

    def first_stage(place):
        def run(block, own):
            far = [from_class(block, place, 8, 8)]
            far += [from_class(block, place, 4, hop) for hop in (4, -4)]
            return far[0], far[1], far[2], exchange(own)

        return run

    def second_stage(place):
        def run(middle, chunk):
            up = from_class(middle, place, 4, 1)
            down = from_class(middle, place, 4, -1)
            top = from_class(middle[:size], place, 4, 2)
            bottom = from_class(middle[size:], place, 4, -2)
            return up, down, top, bottom, exchange(jnp.tile(chunk, (n_row, 1)))

        return run

    first_stages = [first_stage(place) for place in range(8)]
    second_stages = [second_stage(place) for place in range(4)]

    def fetch(block, first):
        plane = first // 2
        dist = (my_z - plane) % n_z
        root, slot = first % n_row, first // n_row
        own = lax.dynamic_slice_in_dim(block, slot * size, size, 0)
        across, ahead, behind, scattered = lax.switch(plane % 8, first_stages, block, own)
        middle = jnp.where(
            dist == 8,
            across,
            jnp.where(dist == 4, ahead, jnp.where(dist == n_z - 4, behind, block)),
        )
        piece = size // n_row
        chunk = lax.dynamic_slice_in_dim(scattered, root * piece, 2 * piece, 0)
        up, down, top, bottom, gathered = lax.switch(plane % 4, second_stages, middle, chunk)
        near = dist % 4
        columns = jnp.where(
            near == 0,
            middle,
            jnp.where(
                near == 1, up, jnp.where(near == 3, down, jnp.concatenate([top, bottom], axis=0))
            ),
        )
        rows = gathered.reshape(n_row, 2, piece, size).transpose(1, 0, 2, 3).reshape(width, size)
        return columns, rows

    block = matrix
    for step in range(panel_index.shape[0]):
        first = panel_index[step]
        plane = first // 2
        mine, rows = fetch(block, first)
        other = lax.ppermute(mine, "col", [(i, i ^ 1) for i in range(n_col)])
        upper = dot(lower_inv[step], rows)
        u_mine = lax.dynamic_slice_in_dim(upper_inv[step], core * size, size, 0)
        u_other = lax.dynamic_slice_in_dim(upper_inv[step], (1 - core) * size, size, 0)
        lower = dot(mine, u_mine) + dot(other, u_other)
        row_hit = jnp.repeat(row_struct[step] > 0, size)[:, None]
        col_hit = col_struct[step, 0] > 0
        schur = dot(
            jnp.where(row_hit, lower, jnp.float32(0.0)),
            jnp.where(col_hit, upper, jnp.float32(0.0)),
        )
        block = block - schur
        lower_mine = lax.dynamic_slice_in_dim(lower, core * size, size, 1)
        block = jnp.where((my_z == plane) & row_hit, lower_mine, block)
        for member in range(2):
            root, slot = (first + member) % n_row, (first + member) // n_row
            take = jnp.repeat(jnp.arange(2) == slot, size)[:, None] & (my_row == root) & col_hit
            part = upper[member * size : (member + 1) * size]
            block = jnp.where(take, jnp.concatenate([part, part], axis=0), block)
    return block


def solution(mesh):
    return jax.shard_map(
        local,
        mesh=mesh,
        in_specs=(P("row", "col"), P(None, "row"), P(None, "col"), P(), P(), P()),
        out_specs=P("row", "col"),
        check_vma=False,
    )
```

```python
import functools

import jax
import jax.numpy as jnp
from jax import lax
from jax.experimental import pallas as pl
from jax.experimental.pallas import tpu as pltpu
from jax.sharding import PartitionSpec as P

VMEM_BYTES = 40 * 1024 * 1024


def split(value):
    high = value.astype(jnp.bfloat16)
    low = (value - high.astype(jnp.float32)).astype(jnp.bfloat16)
    return high, low


def dot(a, b):
    (a_high, a_low), (b_high, b_low) = a, b
    mul = functools.partial(jnp.dot, preferred_element_type=jnp.float32)
    return mul(a_high, b_high) + (mul(a_high, b_low) + mul(a_low, b_high))


def early_kernel(n_row, gathered_ref, mine_ref, lower_ref, upper_ref, rows_out, cols_out, rows):
    size = rows.shape[1]
    piece = size // n_row
    for r in range(n_row):
        at = 2 * piece * r
        rows[piece * r : piece * (r + 1)] = gathered_ref[at : at + piece]
        rows[size + piece * r : size + piece * (r + 1)] = gathered_ref[
            at + piece : at + 2 * piece
        ]
    half = pl.ds(pl.multiple_of(lax.axis_index("col") % 2 * size, size), size)
    rows_out[...] = dot(split(lower_ref[0]), split(rows[...]))
    cols_out[...] = dot(split(mine_ref[...]), split(upper_ref[0, half]))


def late_kernel(
    n_row,
    step,
    row_struct,
    col_struct,
    panel,
    other_ref,
    part_ref,
    rows_ref,
    upper_ref,
    block_ref,
    out_ref,
    cols,
):
    size = rows_ref.shape[1]
    my_row, my_col = lax.axis_index("row"), lax.axis_index("col")
    core = my_col % 2
    first = panel[step]
    half = pl.ds(pl.multiple_of((1 - core) * size, size), size)
    cols[...] = part_ref[...] + dot(split(other_ref[...]), split(upper_ref[0, half]))
    col_hit = col_struct[step, 0] > 0
    rows = rows_ref[...]
    kept = split(jnp.where(col_hit, rows, jnp.float32(0.0)))
    owner = my_col // 2 == first // 2
    for slot in range(2):
        at = slice(slot * size, (slot + 1) * size)
        row_hit = row_struct[step, slot] > 0
        whole = cols[at]
        masked = jnp.where(row_hit, whole, jnp.float32(0.0))
        new = block_ref[at] - dot(split(masked), kept)
        own = jnp.where(core == 0, whole[:, :size], whole[:, size:])
        new = jnp.where(owner & row_hit, own, new)
        for member in range(2):
            here = (my_row == (first + member) % n_row) & (slot == first // n_row) & col_hit
            new = jnp.where(here, rows[member * size : (member + 1) * size], new)
        out_ref[at] = new


def local(matrix, row_struct, col_struct, panel_index, lower_inv, upper_inv):
    n_row = lax.axis_size("row")
    n_col = lax.axis_size("col")
    n_z = n_col // 2
    my_col = lax.axis_index("col")
    my_z = my_col // 2
    width = upper_inv.shape[1]
    size = width // 2
    piece = size // n_row

    def send_z(value, hops):
        pairs = [(2 * (a % n_z) + c, 2 * (b % n_z) + c) for a, b in hops for c in range(2)]
        return lax.ppermute(value, "col", pairs)

    def from_class(value, place, spacing, hop):
        return send_z(value, [(z, z + hop) for z in range(place % spacing, n_z, spacing)])

    def exchange(value):
        return lax.all_to_all(value, "row", 0, 0, tiled=True)

    def first_stage(place):
        def run(block, first):
            dist = (my_z - first // 2) % n_z
            across = from_class(block, place, 8, 8)
            ahead = from_class(block, place, 4, 4)
            behind = from_class(block, place, 4, -4)
            own = lax.dynamic_slice_in_dim(block, first // n_row * size, size, 0)
            scattered = exchange(own)
            chunk = lax.dynamic_slice_in_dim(scattered, first % n_row * piece, 2 * piece, 0)
            middle = jnp.where(
                dist == 8,
                across,
                jnp.where(dist == 4, ahead, jnp.where(dist == n_z - 4, behind, block)),
            )
            return middle, chunk

        return run

    def second_stage(place):
        def run(middle, chunk, first):
            near = (my_z - first // 2) % 4
            up = from_class(middle, place, 4, 1)
            down = from_class(middle, place, 4, -1)
            halves = lax.optimization_barrier((middle[:size], middle[size:], chunk))
            top = from_class(halves[0], place, 4, 2)
            bottom = from_class(halves[1], place, 4, -2)
            gathered = exchange(jnp.tile(halves[2], (n_row, 1)))
            both = jnp.concatenate([top, bottom], axis=0)
            columns = jnp.where(
                near == 0, middle, jnp.where(near == 1, up, jnp.where(near == 3, down, both))
            )
            return columns, gathered

        return run

    first_stages = [first_stage(place) for place in range(8)]
    second_stages = [second_stage(place) for place in range(4)]
    whole = pl.BlockSpec(memory_space=pltpu.VMEM)
    scalars = pl.BlockSpec(memory_space=pltpu.SMEM)
    params = pltpu.CompilerParams(vmem_limit_bytes=VMEM_BYTES)
    f32 = jnp.float32

    block = matrix
    for step in range(panel_index.shape[0]):
        first = panel_index[step]
        plane = first // 2
        matrix_of = pl.BlockSpec((1, width, width), lambda i, step=step: (step, 0, 0))
        middle, chunk = lax.switch(plane % 8, first_stages, block, first)
        mine, gathered = lax.switch(plane % 4, second_stages, middle, chunk, first)
        other = lax.ppermute(mine, "col", [(i, i ^ 1) for i in range(n_col)])
        rows, part = pl.pallas_call(
            functools.partial(early_kernel, n_row),
            grid=(1,),
            out_shape=(
                jax.ShapeDtypeStruct((width, size), f32),
                jax.ShapeDtypeStruct((2 * size, width), f32),
            ),
            in_specs=[whole, whole, matrix_of, matrix_of],
            out_specs=(whole, whole),
            scratch_shapes=[pltpu.VMEM((width, size), f32)],
            compiler_params=params,
            cost_estimate=pl.CostEstimate(
                flops=6 * width * width * width, bytes_accessed=12 * width * width, transcendentals=0
            ),
            name="early",
        )(gathered, mine, lower_inv, upper_inv)
        block = pl.pallas_call(
            functools.partial(late_kernel, n_row, step),
            grid=(1,),
            out_shape=jax.ShapeDtypeStruct(matrix.shape, f32),
            in_specs=[scalars, scalars, scalars, whole, whole, whole, matrix_of, whole],
            out_specs=whole,
            scratch_shapes=[pltpu.VMEM((2 * size, width), f32)],
            compiler_params=params,
            cost_estimate=pl.CostEstimate(
                flops=6 * width * width * width, bytes_accessed=12 * width * width, transcendentals=0
            ),
            name="late",
        )(row_struct, col_struct, panel_index, other, part, rows, upper_inv, block)
    return block


def solution(mesh):
    return jax.shard_map(
        local,
        mesh=mesh,
        in_specs=(P("row", "col"), P(None, "row"), P(None, "col"), P(), P(), P()),
        out_specs=P("row", "col"),
        check_vma=False,
    )
```

```python
import functools

import jax
import jax.numpy as jnp
from jax import lax
from jax.experimental import pallas as pl
from jax.experimental.pallas import tpu as pltpu
from jax.sharding import PartitionSpec as P

VMEM_BYTES = 40 * 1024 * 1024


def split(value):
    high = value.astype(jnp.bfloat16)
    low = (value - high.astype(jnp.float32)).astype(jnp.bfloat16)
    return high, low


def dot(a, b):
    (a_high, a_low), (b_high, b_low) = a, b
    mul = functools.partial(jnp.dot, preferred_element_type=jnp.float32)
    return mul(a_high, b_high) + (mul(a_high, b_low) + mul(a_low, b_high))


def early_kernel(
    n_row,
    step,
    gathered_ref,
    mine_ref,
    lower_ref,
    upper_ref,
    rows_out,
    cols_out,
    upper_out,
    rows,
    lower,
    upper,
    sems,
):
    size = rows.shape[1]
    piece = size // n_row
    core = lax.axis_index("col") & 1
    near = pl.ds(pl.multiple_of(core * size, size), size)
    far = pl.ds(pl.multiple_of((1 - core) * size, size), size)
    copies = [
        pltpu.make_async_copy(upper_ref.at[step, near], upper, sems.at[0]),
        pltpu.make_async_copy(lower_ref.at[step], lower, sems.at[1]),
        pltpu.make_async_copy(upper_ref.at[step, far], upper_out, sems.at[2]),
    ]
    for copy in copies:
        copy.start()
    for r in range(n_row):
        at = 2 * piece * r
        rows[piece * r : piece * (r + 1)] = gathered_ref[at : at + piece]
        rows[size + piece * r : size + piece * (r + 1)] = gathered_ref[
            at + piece : at + 2 * piece
        ]
    copies[0].wait()
    cols_out[...] = dot(split(mine_ref[...]), split(upper[...]))
    copies[1].wait()
    rows_out[...] = dot(split(lower[...]), split(rows[...]))
    copies[2].wait()


def late_kernel(
    n_row, step, flags, other_ref, part_ref, rows_ref, upper_ref, block_ref, out_ref, cols
):
    size = rows_ref.shape[1]
    my_row, my_col = lax.axis_index("row"), lax.axis_index("col")
    core = my_col & 1
    first = flags[6 + step]
    cols[...] = part_ref[...] + dot(split(other_ref[...]), split(upper_ref[...]))
    col_hit = flags[4 + step] > 0
    rows = rows_ref[...]
    kept = split(jnp.where(col_hit, rows, jnp.float32(0.0)))
    owner = (my_col >> 1) == (first >> 1)
    for slot in range(2):
        at = slice(slot * size, (slot + 1) * size)
        row_hit = flags[2 * step + slot] > 0
        whole = cols[at]
        masked = jnp.where(row_hit, whole, jnp.float32(0.0))
        new = block_ref[at] - dot(split(masked), kept)
        own = jnp.where(core == 0, whole[:, :size], whole[:, size:])
        new = jnp.where(owner & row_hit, own, new)
        for member in range(2):
            here = (
                (my_row == lax.rem(first + member, n_row))
                & (slot == lax.div(first, n_row))
                & col_hit
            )
            new = jnp.where(here, rows[member * size : (member + 1) * size], new)
        out_ref[at] = new


def local(matrix, row_struct, col_struct, panel_index, lower_inv, upper_inv):
    n_row = lax.axis_size("row")
    n_col = lax.axis_size("col")
    n_z = n_col // 2
    my_z = lax.axis_index("col") >> 1
    width = upper_inv.shape[1]
    size = width // 2
    piece = size // n_row

    def send_z(value, hops):
        pairs = [(2 * (a % n_z) + c, 2 * (b % n_z) + c) for a, b in hops for c in range(2)]
        return lax.ppermute(value, "col", pairs)

    def from_class(value, place, spacing, hop):
        return send_z(value, [(z, z + hop) for z in range(place % spacing, n_z, spacing)])

    def exchange(value):
        return lax.all_to_all(value, "row", 0, 0, tiled=True)

    def fetch(place):
        def run(block, chunk_at, own_at, dist, near):
            across = from_class(block, place, 8, 8)
            ahead = from_class(block, place, 4, 4)
            behind = from_class(block, place, 4, -4)
            own = lax.dynamic_slice_in_dim(block, own_at, size, 0)
            chunk = lax.dynamic_slice_in_dim(exchange(own), chunk_at, 2 * piece, 0)
            tiled, anchor = lax.optimization_barrier((jnp.tile(chunk, (n_row, 1)), block))
            gathered = exchange(tiled)
            middle = jnp.where(
                dist == 8,
                across,
                jnp.where(dist == 4, ahead, jnp.where(dist == n_z - 4, behind, anchor)),
            )
            up = from_class(middle, place, 4, 1)
            down = from_class(middle, place, 4, -1)
            top = from_class(middle[:size], place, 4, 2)
            bottom = from_class(middle[size:], place, 4, -2)
            both = jnp.concatenate([top, bottom], axis=0)
            columns = jnp.where(
                near == 0, middle, jnp.where(near == 1, up, jnp.where(near == 3, down, both))
            )
            return columns, gathered

        return run

    fetches = [fetch(place) for place in range(8)]
    whole = pl.BlockSpec(memory_space=pltpu.VMEM)
    scalars = pl.BlockSpec(memory_space=pltpu.SMEM)
    outside = pl.BlockSpec(memory_space=pltpu.HBM)
    params = pltpu.CompilerParams(vmem_limit_bytes=VMEM_BYTES)
    cost = pl.CostEstimate(
        flops=6 * width * width * width, bytes_accessed=12 * width * width, transcendentals=0
    )
    f32 = jnp.float32
    flags = jnp.concatenate([row_struct.reshape(-1), col_struct.reshape(-1), panel_index])

    places = []
    for step in range(panel_index.shape[0]):
        first = panel_index[step]
        plane = first >> 1
        dist = (my_z - plane) & (n_z - 1)
        places += [
            plane & 7,
            (first & (n_row - 1)) * piece,
            (first >> (n_row.bit_length() - 1)) * size,
            dist,
            dist & 3,
        ]
    flags, places = lax.optimization_barrier((flags, places))

    block = matrix
    for step in range(panel_index.shape[0]):
        which, *at = places[5 * step : 5 * step + 5]
        mine, gathered = lax.switch(which, fetches, block, *at)
        other = lax.ppermute(mine, "col", [(i, i ^ 1) for i in range(n_col)])
        rows, part, upper = pl.pallas_call(
            functools.partial(early_kernel, n_row, step),
            out_shape=(
                jax.ShapeDtypeStruct((width, size), f32),
                jax.ShapeDtypeStruct((2 * size, width), f32),
                jax.ShapeDtypeStruct((size, width), f32),
            ),
            in_specs=[whole, whole, outside, outside],
            out_specs=(whole, whole, whole),
            scratch_shapes=[
                pltpu.VMEM((width, size), f32),
                pltpu.VMEM((width, width), f32),
                pltpu.VMEM((size, width), f32),
                pltpu.SemaphoreType.DMA((3,)),
            ],
            compiler_params=params,
            cost_estimate=cost,
            name="early",
        )(gathered, mine, lower_inv, upper_inv)
        block = pl.pallas_call(
            functools.partial(late_kernel, n_row, step),
            out_shape=jax.ShapeDtypeStruct(matrix.shape, f32),
            in_specs=[scalars, whole, whole, whole, whole, whole],
            out_specs=whole,
            scratch_shapes=[pltpu.VMEM((2 * size, width), f32)],
            compiler_params=params,
            cost_estimate=cost,
            name="late",
        )(flags, other, part, rows, upper, block)
    return block


def solution(mesh):
    return jax.shard_map(
        local,
        mesh=mesh,
        in_specs=(P("row", "col"), P(None, "row"), P(None, "col"), P(), P(), P()),
        out_specs=P("row", "col"),
        check_vma=False,
    )
```

```python
import functools

import jax
import jax.numpy as jnp
from jax import lax
from jax.experimental import pallas as pl
from jax.experimental.pallas import tpu as pltpu
from jax.sharding import PartitionSpec as P

VMEM_BYTES = 40 * 1024 * 1024


def split(value):
    high = value.astype(jnp.bfloat16)
    low = (value - high.astype(jnp.float32)).astype(jnp.bfloat16)
    return high, low


def dot(a, b):
    (a_high, a_low), (b_high, b_low) = a, b
    mul = functools.partial(jnp.dot, preferred_element_type=jnp.float32)
    return mul(a_high, b_high) + (mul(a_high, b_low) + mul(a_low, b_high))


def early_kernel(n_row, gathered_ref, mine_ref, lower_ref, upper_ref, rows_out, cols_out, rows):
    size = rows.shape[1]
    piece = size // n_row
    for r in range(n_row):
        at = 2 * piece * r
        rows[piece * r : piece * (r + 1)] = gathered_ref[at : at + piece]
        rows[size + piece * r : size + piece * (r + 1)] = gathered_ref[
            at + piece : at + 2 * piece
        ]
    half = pl.ds(pl.multiple_of((lax.axis_index("col") & 1) * size, size), size)
    rows_out[...] = dot(split(lower_ref[...]), split(rows[...]))
    cols_out[...] = dot(split(mine_ref[...]), split(upper_ref[half]))


def late_kernel(
    n_row, step, flags, other_ref, part_ref, rows_ref, upper_ref, block_ref, out_ref, cols
):
    size = rows_ref.shape[1]
    my_row, my_col = lax.axis_index("row"), lax.axis_index("col")
    core = my_col & 1
    first = flags[6 + step]
    half = pl.ds(pl.multiple_of((1 - core) * size, size), size)
    cols[...] = part_ref[...] + dot(split(other_ref[...]), split(upper_ref[half]))
    col_hit = flags[4 + step] > 0
    rows = rows_ref[...]
    kept = split(jnp.where(col_hit, rows, jnp.float32(0.0)))
    owner = (my_col >> 1) == (first >> 1)
    for slot in range(2):
        at = slice(slot * size, (slot + 1) * size)
        row_hit = flags[2 * step + slot] > 0
        whole = cols[at]
        masked = jnp.where(row_hit, whole, jnp.float32(0.0))
        new = block_ref[at] - dot(split(masked), kept)
        own = jnp.where(core == 0, whole[:, :size], whole[:, size:])
        new = jnp.where(owner & row_hit, own, new)
        for member in range(2):
            here = (
                (my_row == lax.rem(first + member, n_row))
                & (slot == lax.div(first, n_row))
                & col_hit
            )
            new = jnp.where(here, rows[member * size : (member + 1) * size], new)
        out_ref[at] = new


def local(matrix, row_struct, col_struct, panel_index, lower_inv, upper_inv):
    n_row = lax.axis_size("row")
    n_col = lax.axis_size("col")
    n_z = n_col // 2
    my_z = lax.axis_index("col") >> 1
    width = upper_inv.shape[1]
    size = width // 2
    piece = size // n_row

    def send_z(value, hops):
        pairs = [(2 * (a % n_z) + c, 2 * (b % n_z) + c) for a, b in hops for c in range(2)]
        return lax.ppermute(value, "col", pairs)

    def from_class(value, place, spacing, hop):
        return send_z(value, [(z, z + hop) for z in range(place % spacing, n_z, spacing)])

    def exchange(value):
        return lax.all_to_all(value, "row", 0, 0, tiled=True)

    def to_leaders(place):
        hops = [hop if hop >= -7 else 8 for hop in (3 - place, 7 - place, -1 - place, -5 - place)]

        def run(block, chunk_at, own, dist, plane):
            quarter = None
            for n, hop in enumerate(hops):
                at = (((plane >> 2) + (0, 1, 3, 2)[n]) & 3) * part_rows
                part = lax.dynamic_slice_in_dim(block, at, part_rows, 0)
                got = part if hop == 0 else from_class(part, place, 4, hop)
                quarter = got if n == 0 else jnp.where(dist == hop % n_z, got, quarter)
            chunk = lax.dynamic_slice_in_dim(exchange(own), chunk_at, 2 * piece, 0)
            return quarter, chunk

        return run

    def fetch(block, inverses, which, chunk_at, own_at, dist, plane):
        own = lax.dynamic_slice_in_dim(block, own_at, size, 0)
        quarter, chunk = lax.switch(which, leads, block, chunk_at, own, dist, plane)
        around = [quarter] + [from_class(quarter, 3, 4, hop) for hop in (-4, 8, 4)]
        middle = jnp.zeros((4,) + quarter.shape, quarter.dtype)
        for n in range(4):
            middle = lax.dynamic_update_index_in_dim(
                middle, around[n], ((my_z >> 2) + n) & 3, 0
            )
        middle = middle.reshape(block.shape)
        up = from_class(middle, 3, 4, 1)
        down = from_class(middle, 3, 4, -1)
        top = from_class(middle[:size], 3, 4, 2)
        bottom = from_class(middle[size:], 3, 4, -2)
        gathered = exchange(jnp.tile(chunk, (n_row, 1)))
        near = my_z & 3
        up, inverses = lax.optimization_barrier((up, inverses))
        both = jnp.concatenate([top, bottom], axis=0)
        columns = jnp.where(
            near == 3, middle, jnp.where(near == 0, up, jnp.where(near == 2, down, both))
        )
        return columns, gathered, inverses

    part_rows = matrix.shape[0] // 4
    leads = [to_leaders(place) for place in range(4)]
    whole = pl.BlockSpec(memory_space=pltpu.VMEM)
    scalars = pl.BlockSpec(memory_space=pltpu.SMEM)
    params = pltpu.CompilerParams(vmem_limit_bytes=VMEM_BYTES)
    cost = pl.CostEstimate(
        flops=6 * width * width * width, bytes_accessed=12 * width * width, transcendentals=0
    )
    f32 = jnp.float32
    flags = jnp.concatenate([row_struct.reshape(-1), col_struct.reshape(-1), panel_index])

    places = []
    for step in range(panel_index.shape[0]):
        first = panel_index[step]
        plane = first >> 1
        dist = (my_z - plane) & (n_z - 1)
        places += [
            plane & 3,
            (first & (n_row - 1)) * piece,
            (first >> (n_row.bit_length() - 1)) * size,
            dist,
            plane,
        ]
    flags, places = lax.optimization_barrier((flags, places))

    block = matrix
    for step in range(panel_index.shape[0]):
        inverses = lower_inv[step], upper_inv[step]
        mine, gathered, (lower, upper) = fetch(block, inverses, *places[5 * step : 5 * step + 5])
        other = lax.ppermute(mine, "col", [(i, i ^ 1) for i in range(n_col)])
        rows, part = pl.pallas_call(
            functools.partial(early_kernel, n_row),
            out_shape=(
                jax.ShapeDtypeStruct((width, size), f32),
                jax.ShapeDtypeStruct((2 * size, width), f32),
            ),
            in_specs=[whole] * 4,
            out_specs=(whole, whole),
            scratch_shapes=[pltpu.VMEM((width, size), f32)],
            compiler_params=params,
            cost_estimate=cost,
            name="early",
        )(gathered, mine, lower, upper)
        block = pl.pallas_call(
            functools.partial(late_kernel, n_row, step),
            out_shape=jax.ShapeDtypeStruct(matrix.shape, f32),
            in_specs=[scalars] + [whole] * 5,
            out_specs=whole,
            scratch_shapes=[pltpu.VMEM((2 * size, width), f32)],
            compiler_params=params,
            cost_estimate=cost,
            name="late",
        )(flags, other, part, rows, upper, block)
    return block


def solution(mesh):
    return jax.shard_map(
        local,
        mesh=mesh,
        in_specs=(P("row", "col"), P(None, "row"), P(None, "col"), P(), P(), P()),
        out_specs=P("row", "col"),
        check_vma=False,
    )
```

```python
import functools

import jax
import jax.numpy as jnp
from jax import lax
from jax.experimental import pallas as pl
from jax.experimental.pallas import tpu as pltpu
from jax.sharding import PartitionSpec as P

VMEM_BYTES = 20 * 1024 * 1024


def split(value):
    high = value.astype(jnp.bfloat16)
    low = (value - high.astype(jnp.float32)).astype(jnp.bfloat16)
    return high, low


def dot(a, b):
    (a_high, a_low), (b_high, b_low) = a, b
    mul = functools.partial(jnp.dot, preferred_element_type=jnp.float32)
    return mul(a_high, b_high) + (mul(a_high, b_low) + mul(a_low, b_high))


def early_kernel(n_row, gathered_ref, mine_ref, lower_ref, upper_ref, rows_out, cols_out, rows):
    size = rows.shape[1]
    piece = size // n_row
    for r in range(n_row):
        at = 2 * piece * r
        rows[piece * r : piece * (r + 1)] = gathered_ref[at : at + piece]
        rows[size + piece * r : size + piece * (r + 1)] = gathered_ref[
            at + piece : at + 2 * piece
        ]
    half = pl.ds(pl.multiple_of((lax.axis_index("col") & 1) * size, size), size)
    rows_out[...] = dot(split(lower_ref[...]), split(rows[...]))
    cols_out[...] = dot(split(mine_ref[...]), split(upper_ref[half]))


def late_kernel(
    n_row, step, flags, other_ref, part_ref, rows_ref, upper_ref, block_ref, out_ref, cols
):
    size = rows_ref.shape[1]
    my_row, my_col = lax.axis_index("row"), lax.axis_index("col")
    core = my_col & 1
    first = flags[6 + step]
    half = pl.ds(pl.multiple_of((1 - core) * size, size), size)
    cols[...] = part_ref[...] + dot(split(other_ref[...]), split(upper_ref[half]))
    col_hit = flags[4 + step] > 0
    rows = rows_ref[...]
    kept = split(jnp.where(col_hit, rows, jnp.float32(0.0)))
    owner = (my_col >> 1) == (first >> 1)
    for slot in range(2):
        at = slice(slot * size, (slot + 1) * size)
        row_hit = flags[2 * step + slot] > 0
        whole = cols[at]
        masked = jnp.where(row_hit, whole, jnp.float32(0.0))
        new = block_ref[at] - dot(split(masked), kept)
        own = jnp.where(core == 0, whole[:, :size], whole[:, size:])
        new = jnp.where(owner & row_hit, own, new)
        for member in range(2):
            here = (
                (my_row == lax.rem(first + member, n_row))
                & (slot == lax.div(first, n_row))
                & col_hit
            )
            new = jnp.where(here, rows[member * size : (member + 1) * size], new)
        out_ref[at] = new


def local(matrix, row_struct, col_struct, panel_index, lower_inv, upper_inv):
    n_row = lax.axis_size("row")
    n_col = lax.axis_size("col")
    n_z = n_col // 2
    my_z = lax.axis_index("col") >> 1
    width = upper_inv.shape[1]
    size = width // 2
    piece = size // n_row

    def send_z(value, hops):
        pairs = [(2 * (a % n_z) + c, 2 * (b % n_z) + c) for a, b in hops for c in range(2)]
        return lax.ppermute(value, "col", pairs)

    def from_class(value, place, spacing, hop):
        return send_z(value, [(z, z + hop) for z in range(place % spacing, n_z, spacing)])

    def exchange(value):
        return lax.all_to_all(value, "row", 0, 0, tiled=True)

    def to_leaders(sends):
        def run(block, chunk_at, own_at, dist):
            got = [from_class(block, place, spacing, hop) for place, spacing, hop in sends]
            own = lax.dynamic_slice_in_dim(block, own_at, size, 0)
            chunk = lax.dynamic_slice_in_dim(exchange(own), chunk_at, 2 * piece, 0)
            tiled, middle = lax.optimization_barrier((jnp.tile(chunk, (n_row, 1)), block))
            for (_, _, hop), value in zip(sends, got):
                middle = jnp.where(dist == hop % n_z, value, middle)
            return middle, middle[:size], middle[size:], tiled

        return run

    def fetch(block, later, which, chunk_at, own_at, dist):
        middle, upper_half, lower_half, tiled = lax.switch(which, leads, block, chunk_at, own_at, dist)
        up = from_class(middle, 3, 4, 1)
        down = from_class(middle, 3, 4, -1)
        top = from_class(upper_half, 3, 4, 2)
        bottom = from_class(lower_half, 3, 4, -2)
        gathered = exchange(tiled)
        near = my_z & 3
        up, later = lax.optimization_barrier((up, later))
        both = jnp.concatenate([top, bottom], axis=0)
        columns = jnp.where(
            near == 3, middle, jnp.where(near == 0, up, jnp.where(near == 2, down, both))
        )
        return columns, gathered, later

    leads = []
    for place in (0, 1, 2, 4, 5, 6):
        hops = [hop - place % 4 for hop in (7, -5, 3, -1)]
        hops.sort(key=abs, reverse=True)
        leads.append(to_leaders([(place, 8 if abs(hop) > 3 else 4, hop) for hop in hops]))
    for place in range(3, n_z, 4):
        leads.append(to_leaders([(place, n_z, hop) for hop in (8, 4, -4)]))
    whole = pl.BlockSpec(memory_space=pltpu.VMEM)
    scalars = pl.BlockSpec(memory_space=pltpu.SMEM)
    params = pltpu.CompilerParams(vmem_limit_bytes=VMEM_BYTES)
    cost = pl.CostEstimate(
        flops=6 * width * width * width, bytes_accessed=12 * width * width, transcendentals=0
    )
    f32 = jnp.float32
    flags = jnp.concatenate([row_struct.reshape(-1), col_struct.reshape(-1), panel_index])

    places = []
    for step in range(panel_index.shape[0]):
        first = panel_index[step]
        plane = first >> 1
        dist = (my_z - plane) & (n_z - 1)
        places += [
            jnp.where(plane & 3 == 3, 6 + (plane >> 2), (plane & 3) + 3 * ((plane & 7) >> 2)),
            (first & (n_row - 1)) * piece,
            (first >> (n_row.bit_length() - 1)) * size,
            dist,
        ]
    places = lax.optimization_barrier(places)

    block = matrix
    for step in range(panel_index.shape[0]):
        later = lower_inv[step], upper_inv[step], flags
        mine, gathered, (lower, upper, flags) = fetch(
            block, later, *places[4 * step : 4 * step + 4]
        )
        other = lax.ppermute(mine, "col", [(i, i ^ 1) for i in range(n_col)])
        rows, part = pl.pallas_call(
            functools.partial(early_kernel, n_row),
            out_shape=(
                jax.ShapeDtypeStruct((width, size), f32),
                jax.ShapeDtypeStruct((2 * size, width), f32),
            ),
            in_specs=[whole] * 4,
            out_specs=(whole, whole),
            scratch_shapes=[pltpu.VMEM((width, size), f32)],
            compiler_params=params,
            cost_estimate=cost,
            name="early",
        )(gathered, mine, lower, upper)
        block = pl.pallas_call(
            functools.partial(late_kernel, n_row, step),
            out_shape=jax.ShapeDtypeStruct(matrix.shape, f32),
            in_specs=[scalars] + [whole] * 5,
            out_specs=whole,
            scratch_shapes=[pltpu.VMEM((2 * size, width), f32)],
            compiler_params=params,
            cost_estimate=cost,
            name="late",
        )(flags, other, part, rows, upper, block)
    return block


def solution(mesh):
    return jax.shard_map(
        local,
        mesh=mesh,
        in_specs=(P("row", "col"), P(None, "row"), P(None, "col"), P(), P(), P()),
        out_specs=P("row", "col"),
        check_vma=False,
    )
```

```python
import functools

import jax
import jax.numpy as jnp
from jax import lax
from jax.experimental import pallas as pl
from jax.experimental.pallas import tpu as pltpu
from jax.sharding import PartitionSpec as P

VMEM_BYTES = 20 * 1024 * 1024


def split(value):
    high = value.astype(jnp.bfloat16)
    low = (value - high.astype(jnp.float32)).astype(jnp.bfloat16)
    return high, low


def dot(a, b):
    (a_high, a_low), (b_high, b_low) = a, b
    mul = functools.partial(jnp.dot, preferred_element_type=jnp.float32)
    return mul(a_high, b_high) + (mul(a_high, b_low) + mul(a_low, b_high))


def early_kernel(n_row, gathered_ref, mine_ref, lower_ref, upper_ref, rows_out, cols_out, rows):
    size = rows.shape[1]
    piece = size // n_row
    for r in range(n_row):
        at = 2 * piece * r
        rows[piece * r : piece * (r + 1)] = gathered_ref[at : at + piece]
        rows[size + piece * r : size + piece * (r + 1)] = gathered_ref[
            at + piece : at + 2 * piece
        ]
    half = pl.ds(pl.multiple_of((lax.axis_index("col") & 1) * size, size), size)
    rows_out[...] = dot(split(lower_ref[...]), split(rows[...]))
    cols_out[...] = dot(split(mine_ref[...]), split(upper_ref[half]))


def late_kernel(
    n_row,
    step,
    n_steps,
    flags,
    other_ref,
    part_ref,
    rows_ref,
    upper_ref,
    block_ref,
    out_ref,
    own_ref,
    cols,
):
    size = rows_ref.shape[1]
    my_row, my_col = lax.axis_index("row"), lax.axis_index("col")
    core = my_col & 1
    first = flags[6 + step]
    half = pl.ds(pl.multiple_of((1 - core) * size, size), size)
    cols[...] = part_ref[...] + dot(split(other_ref[...]), split(upper_ref[half]))
    col_hit = flags[4 + step] > 0
    rows = rows_ref[...]
    kept = split(jnp.where(col_hit, rows, jnp.float32(0.0)))
    owner = (my_col >> 1) == (first >> 1)
    next_slot = lax.div(flags[6 + (step + 1) % n_steps], n_row)
    for slot in range(2):
        at = slice(slot * size, (slot + 1) * size)
        row_hit = flags[2 * step + slot] > 0
        whole = cols[at]
        masked = jnp.where(row_hit, whole, jnp.float32(0.0))
        new = block_ref[at] - dot(split(masked), kept)
        own = jnp.where(core == 0, whole[:, :size], whole[:, size:])
        new = jnp.where(owner & row_hit, own, new)
        for member in range(2):
            here = (
                (my_row == lax.rem(first + member, n_row))
                & (slot == lax.div(first, n_row))
                & col_hit
            )
            new = jnp.where(here, rows[member * size : (member + 1) * size], new)
        out_ref[at] = new

        @pl.when(next_slot == slot)
        def _():
            own_ref[...] = out_ref[at]


def local(matrix, row_struct, col_struct, panel_index, lower_inv, upper_inv):
    n_row = lax.axis_size("row")
    n_col = lax.axis_size("col")
    n_z = n_col // 2
    my_z = lax.axis_index("col") >> 1
    width = upper_inv.shape[1]
    size = width // 2
    piece = size // n_row

    def send_z(value, hops):
        pairs = [(2 * (a % n_z) + c, 2 * (b % n_z) + c) for a, b in hops for c in range(2)]
        return lax.ppermute(value, "col", pairs)

    def from_class(value, place, spacing, hop):
        return send_z(value, [(z, z + hop) for z in range(place % spacing, n_z, spacing)])

    def exchange(value):
        return lax.all_to_all(value, "row", 0, 0, tiled=True)

    def to_leaders(sends):
        def run(block, own, chunk_at, dist):
            got = [from_class(block, place, spacing, hop) for place, spacing, hop in sends]
            chunk = lax.dynamic_slice_in_dim(exchange(own), chunk_at, 2 * piece, 0)
            tiled, middle = lax.optimization_barrier((jnp.tile(chunk, (n_row, 1)), block))
            for (_, _, hop), value in zip(sends, got):
                middle = jnp.where(dist == hop % n_z, value, middle)
            return middle, tiled

        return run

    def fetch(step, block, own, later, which, chunk_at, dist):
        middle, tiled = lax.switch(which, leads, block, own, chunk_at, dist)
        tiled, later = lax.optimization_barrier((tiled, later))
        later = later[0][step], later[1][step], later[2]
        up = from_class(middle, 3, 4, 1)
        down = from_class(middle, 3, 4, -1)
        top = from_class(middle[:size], 3, 4, 2)
        bottom = from_class(middle[size:], 3, 4, -2)
        gathered = exchange(tiled)
        near = my_z & 3
        up, later = lax.optimization_barrier((up, later))
        both = jnp.concatenate([top, bottom], axis=0)
        columns = jnp.where(
            near == 3, middle, jnp.where(near == 0, up, jnp.where(near == 2, down, both))
        )
        return columns, gathered, later

    leads = []
    for place in (0, 1, 2, 4, 5, 6):
        hops = [hop - place % 4 for hop in (7, -5, 3, -1)]
        hops.sort(key=abs, reverse=True)
        leads.append(to_leaders([(place, 8 if abs(hop) > 3 else 4, hop) for hop in hops]))
    for place in range(3, n_z, 4):
        leads.append(to_leaders([(place, n_z, hop) for hop in (8, 4, -4)]))
    whole = pl.BlockSpec(memory_space=pltpu.VMEM)
    scalars = pl.BlockSpec(memory_space=pltpu.SMEM)
    params = pltpu.CompilerParams(vmem_limit_bytes=VMEM_BYTES)
    cost = pl.CostEstimate(
        flops=6 * width * width * width, bytes_accessed=12 * width * width, transcendentals=0
    )
    f32 = jnp.float32
    flags = jnp.concatenate([row_struct.reshape(-1), col_struct.reshape(-1), panel_index])

    places = []
    for step in range(panel_index.shape[0]):
        first = panel_index[step]
        plane = first >> 1
        dist = (my_z - plane) & (n_z - 1)
        places += [
            jnp.where(plane & 3 == 3, 6 + (plane >> 2), (plane & 3) + 3 * ((plane & 7) >> 2)),
            (first & (n_row - 1)) * piece,
            dist,
        ]
    own_at = (panel_index[0] >> (n_row.bit_length() - 1)) * size
    places, own_at = lax.optimization_barrier((places, own_at))
    own = lax.dynamic_slice_in_dim(matrix, own_at, size, 0)

    block = matrix
    for step in range(panel_index.shape[0]):
        later = lower_inv, upper_inv, flags
        mine, gathered, (lower, upper, flags) = fetch(
            step, block, own, later, *places[3 * step : 3 * step + 3]
        )
        other = lax.ppermute(mine, "col", [(i, i ^ 1) for i in range(n_col)])
        rows, part = pl.pallas_call(
            functools.partial(early_kernel, n_row),
            out_shape=(
                jax.ShapeDtypeStruct((width, size), f32),
                jax.ShapeDtypeStruct((2 * size, width), f32),
            ),
            in_specs=[whole] * 4,
            out_specs=(whole, whole),
            scratch_shapes=[pltpu.VMEM((width, size), f32)],
            compiler_params=params,
            cost_estimate=cost,
            name="early",
        )(gathered, mine, lower, upper)
        block, own = pl.pallas_call(
            functools.partial(late_kernel, n_row, step, panel_index.shape[0]),
            out_shape=(
                jax.ShapeDtypeStruct(matrix.shape, f32),
                jax.ShapeDtypeStruct((size, size), f32),
            ),
            in_specs=[scalars] + [whole] * 5,
            out_specs=(whole, whole),
            scratch_shapes=[pltpu.VMEM((2 * size, width), f32)],
            compiler_params=params,
            cost_estimate=cost,
            name="late",
        )(flags, other, part, rows, upper, block)
    return block


def solution(mesh):
    return jax.shard_map(
        local,
        mesh=mesh,
        in_specs=(P("row", "col"), P(None, "row"), P(None, "col"), P(), P(), P()),
        out_specs=P("row", "col"),
        check_vma=False,
    )
```

```python
import functools

import jax
import jax.numpy as jnp
from jax import lax
from jax.experimental import pallas as pl
from jax.experimental.pallas import tpu as pltpu
from jax.sharding import PartitionSpec as P

VMEM_BYTES = 20 * 1024 * 1024


def split(value):
    high = value.astype(jnp.bfloat16)
    low = (value - high.astype(jnp.float32)).astype(jnp.bfloat16)
    return high, low


def dot(a, b):
    (a_high, a_low), (b_high, b_low) = a, b
    mul = functools.partial(jnp.dot, preferred_element_type=jnp.float32)
    return mul(a_high, b_high) + (mul(a_high, b_low) + mul(a_low, b_high))


def early_kernel(n_row, gathered_ref, mine_ref, lower_ref, upper_ref, rows_out, cols_out, rows):
    size = rows.shape[1]
    piece = size // n_row
    for r in range(n_row):
        at = 2 * piece * r
        rows[piece * r : piece * (r + 1)] = gathered_ref[at : at + piece]
        rows[size + piece * r : size + piece * (r + 1)] = gathered_ref[
            at + piece : at + 2 * piece
        ]
    half = pl.ds(pl.multiple_of((lax.axis_index("col") & 1) * size, size), size)
    rows_out[...] = dot(split(lower_ref[...]), split(rows[...]))
    cols_out[...] = dot(split(mine_ref[...]), split(upper_ref[half]))


def late_kernel(
    n_row,
    step,
    n_steps,
    flags,
    other_ref,
    part_ref,
    rows_ref,
    upper_ref,
    block_ref,
    out_ref,
    own_ref,
    cols,
):
    size = rows_ref.shape[1]
    my_row, my_col = lax.axis_index("row"), lax.axis_index("col")
    core = my_col & 1
    first = flags[6 + step]
    half = pl.ds(pl.multiple_of((1 - core) * size, size), size)
    cols[...] = part_ref[...] + dot(split(other_ref[...]), split(upper_ref[half]))
    col_hit = flags[4 + step] > 0
    rows = rows_ref[...]
    kept = split(jnp.where(col_hit, rows, jnp.float32(0.0)))
    owner = (my_col >> 1) == (first >> 1)
    next_slot = lax.div(flags[6 + (step + 1) % n_steps], n_row)
    for slot in range(2):
        at = slice(slot * size, (slot + 1) * size)
        row_hit = flags[2 * step + slot] > 0
        whole = cols[at]
        masked = jnp.where(row_hit, whole, jnp.float32(0.0))
        new = block_ref[at] - dot(split(masked), kept)
        own = jnp.where(core == 0, whole[:, :size], whole[:, size:])
        new = jnp.where(owner & row_hit, own, new)
        for member in range(2):
            here = (
                (my_row == lax.rem(first + member, n_row))
                & (slot == lax.div(first, n_row))
                & col_hit
            )
            new = jnp.where(here, rows[member * size : (member + 1) * size], new)
        out_ref[at] = new

        @pl.when(next_slot == slot)
        def _():
            own_ref[...] = out_ref[at]


def local(matrix, row_struct, col_struct, panel_index, lower_inv, upper_inv):
    n_row = lax.axis_size("row")
    n_col = lax.axis_size("col")
    n_z = n_col // 2
    my_z = lax.axis_index("col") >> 1
    width = upper_inv.shape[1]
    size = width // 2
    piece = size // n_row

    def send_z(value, hops):
        pairs = [(2 * (a % n_z) + c, 2 * (b % n_z) + c) for a, b in hops for c in range(2)]
        return lax.ppermute(value, "col", pairs)

    def from_class(value, place, spacing, hop):
        return send_z(value, [(z, z + hop) for z in range(place % spacing, n_z, spacing)])

    def exchange(value):
        return lax.all_to_all(value, "row", 0, 0, tiled=True)

    def to_leaders(sends):
        def run(block, own, chunk_at, dist):
            got = [from_class(block, place, spacing, hop) for place, spacing, hop in sends]
            if own.ndim == 0:
                own = lax.dynamic_slice_in_dim(block, own, size, 0)
            chunk = lax.dynamic_slice_in_dim(exchange(own), chunk_at, 2 * piece, 0)
            tiled, middle = lax.optimization_barrier((jnp.tile(chunk, (n_row, 1)), block))
            for (_, _, hop), value in zip(sends, got):
                middle = jnp.where(dist == hop % n_z, value, middle)
            return middle, tiled

        return run

    def fetch(step, block, own, later, which, chunk_at, dist):
        middle, tiled = lax.switch(which, leads, block, own, chunk_at, dist)
        tiled, later = lax.optimization_barrier((tiled, later))
        later = later[0][step], later[1][step], later[2]
        up = from_class(middle, 3, 4, 1)
        down = from_class(middle, 3, 4, -1)
        top = from_class(middle[:size], 3, 4, 2)
        bottom = from_class(middle[size:], 3, 4, -2)
        gathered = exchange(tiled)
        near = my_z & 3
        up, later = lax.optimization_barrier((up, later))
        both = jnp.concatenate([top, bottom], axis=0)
        columns = jnp.where(
            near == 3, middle, jnp.where(near == 0, up, jnp.where(near == 2, down, both))
        )
        return columns, gathered, later

    leads = []
    for place in (0, 1, 2, 4, 5, 6):
        hops = [hop - place % 4 for hop in (7, -5, 3, -1)]
        hops.sort(key=abs, reverse=True)
        leads.append(to_leaders([(place, 8 if abs(hop) > 3 else 4, hop) for hop in hops]))
    for place in range(3, n_z, 4):
        leads.append(to_leaders([(place, n_z, hop) for hop in (8, 4, -4)]))
    whole = pl.BlockSpec(memory_space=pltpu.VMEM)
    scalars = pl.BlockSpec(memory_space=pltpu.SMEM)
    params = pltpu.CompilerParams(vmem_limit_bytes=VMEM_BYTES)
    cost = pl.CostEstimate(
        flops=6 * width * width * width, bytes_accessed=12 * width * width, transcendentals=0
    )
    f32 = jnp.float32
    flags = jnp.concatenate([row_struct.reshape(-1), col_struct.reshape(-1), panel_index])

    places = []
    for step in range(panel_index.shape[0]):
        first = panel_index[step]
        plane = first >> 1
        dist = (my_z - plane) & (n_z - 1)
        places += [
            jnp.where(plane & 3 == 3, 6 + (plane >> 2), (plane & 3) + 3 * ((plane & 7) >> 2)),
            (first & (n_row - 1)) * piece,
            dist,
        ]
    own_at = (panel_index[0] >> (n_row.bit_length() - 1)) * size
    places, own = lax.optimization_barrier((places, own_at))

    block = matrix
    for step in range(panel_index.shape[0]):
        later = lower_inv, upper_inv, flags
        mine, gathered, (lower, upper, flags) = fetch(
            step, block, own, later, *places[3 * step : 3 * step + 3]
        )
        other = lax.ppermute(mine, "col", [(i, i ^ 1) for i in range(n_col)])
        rows, part = pl.pallas_call(
            functools.partial(early_kernel, n_row),
            out_shape=(
                jax.ShapeDtypeStruct((width, size), f32),
                jax.ShapeDtypeStruct((2 * size, width), f32),
            ),
            in_specs=[whole] * 4,
            out_specs=(whole, whole),
            scratch_shapes=[pltpu.VMEM((width, size), f32)],
            compiler_params=params,
            cost_estimate=cost,
            name="early",
        )(gathered, mine, lower, upper)
        block, own = pl.pallas_call(
            functools.partial(late_kernel, n_row, step, panel_index.shape[0]),
            out_shape=(
                pltpu.VMEM(matrix.shape, f32),
                pltpu.VMEM((size, size), f32),
            ),
            in_specs=[scalars] + [whole] * 5,
            out_specs=(whole, whole),
            scratch_shapes=[pltpu.VMEM((2 * size, width), f32)],
            compiler_params=params,
            cost_estimate=cost,
            name="late",
        )(flags, other, part, rows, upper, block)
    return block


def solution(mesh):
    return jax.shard_map(
        local,
        mesh=mesh,
        in_specs=(P("row", "col"), P(None, "row"), P(None, "col"), P(), P(), P()),
        out_specs=P("row", "col"),
        check_vma=False,
    )
```

```python
import functools

import jax
import jax.numpy as jnp
from jax import lax
from jax.experimental import pallas as pl
from jax.experimental.pallas import tpu as pltpu
from jax.sharding import PartitionSpec as P

VMEM_BYTES = 20 * 1024 * 1024


def split(value):
    high = value.astype(jnp.bfloat16)
    low = (value - high.astype(jnp.float32)).astype(jnp.bfloat16)
    return high, low


def dot(a, b):
    (a_high, a_low), (b_high, b_low) = a, b
    mul = functools.partial(jnp.dot, preferred_element_type=jnp.float32)
    return mul(a_high, b_high) + (mul(a_high, b_low) + mul(a_low, b_high))


def early_kernel(n_row, gathered_ref, mine_ref, lower_ref, upper_ref, rows_out, cols_out, rows):
    size = rows.shape[1]
    piece = size // n_row
    for r in range(n_row):
        at = 2 * piece * r
        rows[piece * r : piece * (r + 1)] = gathered_ref[at : at + piece]
        rows[size + piece * r : size + piece * (r + 1)] = gathered_ref[
            at + piece : at + 2 * piece
        ]
    half = pl.ds(pl.multiple_of((lax.axis_index("col") & 1) * size, size), size)
    rows_out[...] = dot(split(lower_ref[...]), split(rows[...]))
    cols_out[...] = dot(split(mine_ref[...]), split(upper_ref[half]))


def late_kernel(
    n_row,
    step,
    n_steps,
    flags,
    other_ref,
    part_ref,
    rows_ref,
    upper_ref,
    block_ref,
    out_ref,
    own_ref,
    cols,
    other,
    sems,
):
    size = rows_ref.shape[1]
    my_row, my_col = lax.axis_index("row"), lax.axis_index("col")
    core = my_col & 1
    first = flags[6 + step]
    copies = []
    for slot in range(2):
        at = pl.ds(slot * size, size)
        copies.append(pltpu.make_async_copy(other_ref.at[at], other.at[at], sems.at[slot]))
        copies[slot].start()
    half = pl.ds(pl.multiple_of((1 - core) * size, size), size)
    upper = split(upper_ref[half])
    col_hit = flags[4 + step] > 0
    rows = rows_ref[...]
    kept = split(jnp.where(col_hit, rows, jnp.float32(0.0)))
    owner = (my_col >> 1) == (first >> 1)
    next_slot = lax.div(flags[6 + (step + 1) % n_steps], n_row)
    for slot in range(2):
        at = slice(slot * size, (slot + 1) * size)
        row_hit = flags[2 * step + slot] > 0
        copies[slot].wait()
        cols[at] = part_ref[at] + dot(split(other[at]), upper)
        whole = cols[at]
        masked = jnp.where(row_hit, whole, jnp.float32(0.0))
        new = block_ref[at] - dot(split(masked), kept)
        own = jnp.where(core == 0, whole[:, :size], whole[:, size:])
        new = jnp.where(owner & row_hit, own, new)
        for member in range(2):
            here = (
                (my_row == lax.rem(first + member, n_row))
                & (slot == lax.div(first, n_row))
                & col_hit
            )
            new = jnp.where(here, rows[member * size : (member + 1) * size], new)
        out_ref[at] = new

        @pl.when(next_slot == slot)
        def _():
            own_ref[...] = out_ref[at]


def local(matrix, row_struct, col_struct, panel_index, lower_inv, upper_inv):
    n_row = lax.axis_size("row")
    n_col = lax.axis_size("col")
    n_z = n_col // 2
    my_z = lax.axis_index("col") >> 1
    width = upper_inv.shape[1]
    size = width // 2
    piece = size // n_row

    def send_z(value, hops):
        pairs = [(2 * (a % n_z) + c, 2 * (b % n_z) + c) for a, b in hops for c in range(2)]
        return lax.ppermute(value, "col", pairs)

    def from_class(value, place, spacing, hop):
        return send_z(value, [(z, z + hop) for z in range(place % spacing, n_z, spacing)])

    def exchange(value):
        return lax.all_to_all(value, "row", 0, 0, tiled=True)

    def to_leaders(sends):
        def run(block, own, first):
            dist = (my_z - (first >> 1)) & (n_z - 1)
            got = [from_class(block, place, spacing, hop) for place, spacing, hop in sends]
            if own is None:
                own_at = (first >> (n_row.bit_length() - 1)) * size
                own = lax.dynamic_slice_in_dim(block, own_at.astype(jnp.uint32), size, 0)
            chunk_at = ((first & (n_row - 1)) * piece).astype(jnp.uint32)
            chunk = lax.dynamic_slice_in_dim(exchange(own), chunk_at, 2 * piece, 0)
            tiled, middle = lax.optimization_barrier((jnp.tile(chunk, (n_row, 1)), block))
            for (_, _, hop), value in zip(sends, got):
                middle = jnp.where(dist == hop % n_z, value, middle)
            return middle, tiled

        return run

    def fetch(step, block, own, later):
        first = later[3][step]
        plane = first >> 1
        which = jnp.where(
            plane & 3 == 3, 6 + (plane >> 2), (plane & 3) + 3 * ((plane >> 2) & 1)
        )
        middle, tiled = lax.switch(which, leads, block, own, first)
        tiled, later = lax.optimization_barrier((tiled, later))
        later = later[0][step], later[1][step], later[2], later[3]
        up = from_class(middle, 3, 4, 1)
        down = from_class(middle, 3, 4, -1)
        top = from_class(middle[:size], 3, 4, 2)
        bottom = from_class(middle[size:], 3, 4, -2)
        gathered = exchange(tiled)
        near = my_z & 3
        up, later = lax.optimization_barrier((up, later))
        both = jnp.concatenate([top, bottom], axis=0)
        columns = jnp.where(
            near == 3, middle, jnp.where(near == 0, up, jnp.where(near == 2, down, both))
        )
        return columns, gathered, later

    leads = []
    for place in (0, 1, 2, 4, 5, 6):
        hops = [hop - place % 4 for hop in (7, -5, 3, -1)]
        hops.sort(key=abs, reverse=True)
        leads.append(to_leaders([(place, 8 if abs(hop) > 3 else 4, hop) for hop in hops]))
    for place in range(3, n_z, 4):
        leads.append(to_leaders([(place, n_z, hop) for hop in (8, 4, -4)]))
    whole = pl.BlockSpec(memory_space=pltpu.VMEM)
    scalars = pl.BlockSpec(memory_space=pltpu.SMEM)
    outside = pl.BlockSpec(memory_space=pl.ANY)
    params = pltpu.CompilerParams(vmem_limit_bytes=VMEM_BYTES)
    cost = pl.CostEstimate(
        flops=6 * width * width * width, bytes_accessed=12 * width * width, transcendentals=0
    )
    f32 = jnp.float32
    flags = jnp.concatenate([row_struct.reshape(-1), col_struct.reshape(-1), panel_index])

    block, own, panels = matrix, None, panel_index
    for step in range(panel_index.shape[0]):
        later = lower_inv, upper_inv, flags, panels
        mine, gathered, (lower, upper, flags, panels) = fetch(step, block, own, later)
        other = lax.ppermute(mine, "col", [(i, i ^ 1) for i in range(n_col)])
        rows, part = pl.pallas_call(
            functools.partial(early_kernel, n_row),
            out_shape=(
                jax.ShapeDtypeStruct((width, size), f32),
                jax.ShapeDtypeStruct((2 * size, width), f32),
            ),
            in_specs=[whole] * 4,
            out_specs=(whole, whole),
            scratch_shapes=[pltpu.VMEM((width, size), f32)],
            compiler_params=params,
            cost_estimate=cost,
            name="early",
        )(gathered, mine, lower, upper)
        block, own = pl.pallas_call(
            functools.partial(late_kernel, n_row, step, panel_index.shape[0]),
            out_shape=(
                pltpu.VMEM(matrix.shape, f32),
                pltpu.VMEM((size, size), f32),
            ),
            in_specs=[scalars, outside] + [whole] * 4,
            out_specs=(whole, whole),
            scratch_shapes=[
                pltpu.VMEM((2 * size, width), f32),
                pltpu.VMEM((2 * size, size), f32),
                pltpu.SemaphoreType.DMA((2,)),
            ],
            compiler_params=params,
            cost_estimate=cost,
            name="late",
        )(flags, other, part, rows, upper, block)
    return block


def solution(mesh):
    return jax.shard_map(
        local,
        mesh=mesh,
        in_specs=(P("row", "col"), P(None, "row"), P(None, "col"), P(), P(), P()),
        out_specs=P("row", "col"),
        check_vma=False,
    )
```

```python
import functools

import jax
import jax.numpy as jnp
from jax import lax
from jax.experimental import pallas as pl
from jax.experimental.pallas import tpu as pltpu
from jax.sharding import PartitionSpec as P

VMEM_BYTES = 20 * 1024 * 1024


def split(value):
    high = value.astype(jnp.bfloat16)
    low = (value - high.astype(jnp.float32)).astype(jnp.bfloat16)
    return high, low


def dot(a, b):
    (a_high, a_low), (b_high, b_low) = a, b
    mul = functools.partial(jnp.dot, preferred_element_type=jnp.float32)
    return mul(a_high, b_high) + (mul(a_high, b_low) + mul(a_low, b_high))


def early_kernel(n_row, gathered_ref, mine_ref, lower_ref, upper_ref, rows_out, cols_out, rows):
    size = rows.shape[1]
    piece = size // n_row
    for r in range(n_row):
        at = 2 * piece * r
        rows[piece * r : piece * (r + 1)] = gathered_ref[at : at + piece]
        rows[size + piece * r : size + piece * (r + 1)] = gathered_ref[
            at + piece : at + 2 * piece
        ]
    half = pl.ds(pl.multiple_of((lax.axis_index("col") & 1) * size, size), size)
    rows_out[...] = dot(split(lower_ref[...]), split(rows[...]))
    cols_out[...] = dot(split(mine_ref[...]), split(upper_ref[half]))


def late_kernel(
    n_row,
    step,
    n_steps,
    flags,
    other_ref,
    part_ref,
    rows_ref,
    upper_ref,
    block_ref,
    out_ref,
    *rest,
):
    own_ref, cols = rest if step + 1 < n_steps else (None, *rest)
    size = rows_ref.shape[1]
    my_row, my_col = lax.axis_index("row"), lax.axis_index("col")
    core = my_col & 1
    first = flags[6 + step]
    half = pl.ds(pl.multiple_of((1 - core) * size, size), size)
    cols[...] = part_ref[...] + dot(split(other_ref[...]), split(upper_ref[half]))
    col_hit = flags[4 + step] > 0
    rows = rows_ref[...]
    kept = split(jnp.where(col_hit, rows, jnp.float32(0.0)))
    owner = (my_col >> 1) == (first >> 1)
    next_slot = lax.div(flags[6 + (step + 1) % n_steps], n_row)
    for slot in range(2):
        at = slice(slot * size, (slot + 1) * size)
        row_hit = flags[2 * step + slot] > 0
        whole = cols[at]
        masked = jnp.where(row_hit, whole, jnp.float32(0.0))
        new = block_ref[at] - dot(split(masked), kept)
        own = jnp.where(core == 0, whole[:, :size], whole[:, size:])
        new = jnp.where(owner & row_hit, own, new)
        for member in range(2):
            here = (
                (my_row == lax.rem(first + member, n_row))
                & (slot == lax.div(first, n_row))
                & col_hit
            )
            new = jnp.where(here, rows[member * size : (member + 1) * size], new)
        out_ref[at] = new

        if own_ref is not None:

            @pl.when(next_slot == slot)
            def _():
                own_ref[...] = out_ref[at]


def local(matrix, row_struct, col_struct, panel_index, lower_inv, upper_inv):
    n_row = lax.axis_size("row")
    n_col = lax.axis_size("col")
    n_z = n_col // 2
    my_z = lax.axis_index("col") >> 1
    width = upper_inv.shape[1]
    size = width // 2
    piece = size // n_row

    def send_z(value, hops):
        pairs = [(2 * (a % n_z) + c, 2 * (b % n_z) + c) for a, b in hops for c in range(2)]
        return lax.ppermute(value, "col", pairs)

    def from_class(value, place, spacing, hop):
        return send_z(value, [(z, z + hop) for z in range(place % spacing, n_z, spacing)])

    def exchange(value):
        return lax.all_to_all(value, "row", 0, 0, tiled=True)

    def to_leaders(sends):
        def run(block, own, first):
            dist = (my_z - (first >> 1)) & (n_z - 1)
            got = [from_class(block, place, spacing, hop) for place, spacing, hop in sends]
            if own is None:
                own_at = (first >> (n_row.bit_length() - 1)) * size
                own = lax.dynamic_slice_in_dim(block, own_at.astype(jnp.uint32), size, 0)
            chunk_at = ((first & (n_row - 1)) * piece).astype(jnp.uint32)
            chunk = lax.dynamic_slice_in_dim(exchange(own), chunk_at, 2 * piece, 0)
            tiled, middle = lax.optimization_barrier((jnp.tile(chunk, (n_row, 1)), block))
            for (_, _, hop), value in zip(sends, got):
                middle = jnp.where(dist == hop % n_z, value, middle)
            return middle, tiled

        return run

    def fetch(step, block, own, later):
        first = later[3][step]
        plane = first >> 1
        which = jnp.where(
            plane & 3 == 3, 6 + (plane >> 2), (plane & 3) + 3 * ((plane >> 2) & 1)
        )
        middle, tiled = lax.switch(which, leads, block, own, first)
        tiled, later = lax.optimization_barrier((tiled, later))
        later = later[0][step], later[1][step], later[2], later[3]
        up = from_class(middle, 3, 4, 1)
        down = from_class(middle, 3, 4, -1)
        top = from_class(middle[:size], 3, 4, 2)
        bottom = from_class(middle[size:], 3, 4, -2)
        gathered = exchange(tiled)
        near = my_z & 3
        up, later = lax.optimization_barrier((up, later))
        both = jnp.concatenate([top, bottom], axis=0)
        columns = jnp.where(
            near == 3, middle, jnp.where(near == 0, up, jnp.where(near == 2, down, both))
        )
        return columns, gathered, later

    leads = []
    for place in (0, 1, 2, 4, 5, 6):
        hops = [hop - place % 4 for hop in (7, -5, 3, -1)]
        hops.sort(key=abs, reverse=True)
        leads.append(to_leaders([(place, 8 if abs(hop) > 3 else 4, hop) for hop in hops]))
    for place in range(3, n_z, 4):
        leads.append(to_leaders([(place, n_z, hop) for hop in (8, 4, -4)]))
    whole = pl.BlockSpec(memory_space=pltpu.VMEM)
    scalars = pl.BlockSpec(memory_space=pltpu.SMEM)
    params = pltpu.CompilerParams(vmem_limit_bytes=VMEM_BYTES)
    cost = pl.CostEstimate(
        flops=6 * width * width * width, bytes_accessed=12 * width * width, transcendentals=0
    )
    f32 = jnp.float32
    flags = jnp.concatenate([row_struct.reshape(-1), col_struct.reshape(-1), panel_index])

    block, own, panels = matrix, None, panel_index
    for step in range(panel_index.shape[0]):
        later = lower_inv, upper_inv, flags, panels
        mine, gathered, (lower, upper, flags, panels) = fetch(step, block, own, later)
        other = lax.ppermute(mine, "col", [(i, i ^ 1) for i in range(n_col)])
        rows, part = pl.pallas_call(
            functools.partial(early_kernel, n_row),
            out_shape=(
                jax.ShapeDtypeStruct((width, size), f32),
                jax.ShapeDtypeStruct((2 * size, width), f32),
            ),
            in_specs=[whole] * 4,
            out_specs=(whole, whole),
            scratch_shapes=[pltpu.VMEM((width, size), f32)],
            compiler_params=params,
            cost_estimate=cost,
            name="early",
        )(gathered, mine, lower, upper)
        n_steps = panel_index.shape[0]
        n_out = 2 if step + 1 < n_steps else 1
        block, *own = pl.pallas_call(
            functools.partial(late_kernel, n_row, step, n_steps),
            out_shape=(
                jax.ShapeDtypeStruct(matrix.shape, f32),
                jax.ShapeDtypeStruct((size, size), f32),
            )[:n_out],
            in_specs=[scalars] + [whole] * 5,
            out_specs=(whole, whole)[:n_out],
            scratch_shapes=[
                pltpu.VMEM((2 * size, width), f32),
            ],
            compiler_params=params,
            cost_estimate=cost,
            name="late",
        )(flags, other, part, rows, upper, block)
        own = own[0] if own else None
    return block


def solution(mesh):
    return jax.shard_map(
        local,
        mesh=mesh,
        in_specs=(P("row", "col"), P(None, "row"), P(None, "col"), P(), P(), P()),
        out_specs=P("row", "col"),
        check_vma=False,
    )
```

```python
import functools

import jax
import jax.numpy as jnp
from jax import lax
from jax.experimental import pallas as pl
from jax.experimental.pallas import tpu as pltpu
from jax.sharding import PartitionSpec as P

VMEM_BYTES = 20 * 1024 * 1024


def split(value):
    high = value.astype(jnp.bfloat16)
    low = (value - high.astype(jnp.float32)).astype(jnp.bfloat16)
    return high, low


def dot(a, b):
    (a_high, a_low), (b_high, b_low) = a, b
    mul = functools.partial(jnp.dot, preferred_element_type=jnp.float32)
    return mul(a_high, b_high) + (mul(a_high, b_low) + mul(a_low, b_high))


def early_kernel(n_row, gathered_ref, mine_ref, lower_ref, upper_ref, rows_out, cols_out, rows):
    size = rows.shape[1]
    piece = size // n_row
    for r in range(n_row):
        at = 2 * piece * r
        rows[piece * r : piece * (r + 1)] = gathered_ref[at : at + piece]
        rows[size + piece * r : size + piece * (r + 1)] = gathered_ref[
            at + piece : at + 2 * piece
        ]
    half = pl.ds(pl.multiple_of((lax.axis_index("col") & 1) * size, size), size)
    rows_out[...] = dot(split(lower_ref[...]), split(rows[...]))
    cols_out[...] = dot(split(mine_ref[...]), split(upper_ref[half]))


def late_kernel(
    n_row,
    step,
    n_steps,
    flags,
    other_ref,
    part_ref,
    rows_ref,
    upper_ref,
    block_ref,
    out_ref,
    *rest,
):
    own_ref, cols = rest if step + 1 < n_steps else (None, *rest)
    size = rows_ref.shape[1]
    my_row, my_col = lax.axis_index("row"), lax.axis_index("col")
    core = my_col & 1
    first = flags[6 + step]
    half = pl.ds(pl.multiple_of((1 - core) * size, size), size)
    cols[...] = part_ref[...] + dot(split(other_ref[...]), split(upper_ref[half]))
    col_hit = flags[4 + step] > 0
    rows = rows_ref[...]
    kept = split(jnp.where(col_hit, rows, jnp.float32(0.0)))
    owner = (my_col >> 1) == (first >> 1)
    next_slot = lax.div(flags[6 + (step + 1) % n_steps], n_row)
    for slot in range(2):
        at = slice(slot * size, (slot + 1) * size)
        row_hit = flags[2 * step + slot] > 0
        whole = cols[at]
        masked = jnp.where(row_hit, whole, jnp.float32(0.0))
        new = block_ref[at] - dot(split(masked), kept)
        own = jnp.where(core == 0, whole[:, :size], whole[:, size:])
        new = jnp.where(owner & row_hit, own, new)
        for member in range(2):
            here = (
                (my_row == lax.rem(first + member, n_row))
                & (slot == lax.div(first, n_row))
                & col_hit
            )
            new = jnp.where(here, rows[member * size : (member + 1) * size], new)
        out_ref[at] = new

        if own_ref is not None:

            @pl.when(next_slot == slot)
            def _():
                own_ref[...] = out_ref[at]


def local(matrix, row_struct, col_struct, panel_index, lower_inv, upper_inv):
    n_row = lax.axis_size("row")
    n_col = lax.axis_size("col")
    n_z = n_col // 2
    my_z = lax.axis_index("col") >> 1
    width = upper_inv.shape[1]
    size = width // 2
    piece = size // n_row

    def send_z(value, hops):
        pairs = [(2 * (a % n_z) + c, 2 * (b % n_z) + c) for a, b in hops for c in range(2)]
        return lax.ppermute(value, "col", pairs)

    def from_class(value, place, spacing, hop):
        return send_z(value, [(z, z + hop) for z in range(place % spacing, n_z, spacing)])

    def exchange(value):
        return lax.all_to_all(value, "row", 0, 0, tiled=True)

    def to_leaders(sends):
        def run(block, own, first):
            dist = (my_z - (first >> 1)) & (n_z - 1)
            got = [from_class(block, place, spacing, hop) for place, spacing, hop in sends]
            if own is None:
                own_at = (first >> (n_row.bit_length() - 1)) * size
                own = lax.dynamic_slice_in_dim(block, own_at.astype(jnp.uint32), size, 0)
            chunk_at = ((first & (n_row - 1)) * piece).astype(jnp.uint32)
            chunk = lax.dynamic_slice_in_dim(exchange(own), chunk_at, 2 * piece, 0)
            tiled, middle = lax.optimization_barrier((jnp.tile(chunk, (n_row, 1)), block))
            for (_, _, hop), value in zip(sends, got):
                middle = jnp.where(dist == hop % n_z, value, middle)
            return middle, tiled

        return run

    def fetch(step, block, own, later):
        first = later[3][step]
        plane = first >> 1
        which = jnp.where(
            plane & 3 == 3, 6 + (plane >> 2), (plane & 3) + 3 * ((plane >> 2) & 1)
        )
        middle, tiled = lax.switch(which, leads, block, own, first)
        tiled, later = lax.optimization_barrier((tiled, later))
        later = later[0][step], later[1][step], later[2], later[3]
        up = from_class(middle, 3, 4, 1)
        down = from_class(middle, 3, 4, -1)
        top = from_class(middle[:size], 3, 4, 2)
        bottom = from_class(middle[size:], 3, 4, -2)
        gathered = exchange(tiled)
        near = my_z & 3
        up, later = lax.optimization_barrier((up, later))
        both = jnp.concatenate([top, bottom], axis=0)
        columns = jnp.where(
            near == 3, middle, jnp.where(near == 0, up, jnp.where(near == 2, down, both))
        )
        return columns, gathered, later

    leads = []
    for place in (0, 1, 2, 4, 5, 6):
        hops = [hop - place % 4 for hop in (7, -5, 3, -1)]
        hops.sort(key=abs)
        leads.append(to_leaders([(place, 8 if abs(hop) > 3 else 4, hop) for hop in hops]))
    for place in range(3, n_z, 4):
        leads.append(to_leaders([(place, n_z, hop) for hop in (-4, 4, 8)]))
    whole = pl.BlockSpec(memory_space=pltpu.VMEM)
    scalars = pl.BlockSpec(memory_space=pltpu.SMEM)
    params = pltpu.CompilerParams(vmem_limit_bytes=VMEM_BYTES)
    cost = pl.CostEstimate(
        flops=6 * width * width * width, bytes_accessed=12 * width * width, transcendentals=0
    )
    f32 = jnp.float32
    flags = jnp.concatenate([row_struct.reshape(-1), col_struct.reshape(-1), panel_index])

    block, own, panels = matrix, None, panel_index
    for step in range(panel_index.shape[0]):
        later = lower_inv, upper_inv, flags, panels
        mine, gathered, (lower, upper, flags, panels) = fetch(step, block, own, later)
        other = lax.ppermute(mine, "col", [(i, i ^ 1) for i in range(n_col)])
        rows, part = pl.pallas_call(
            functools.partial(early_kernel, n_row),
            out_shape=(
                jax.ShapeDtypeStruct((width, size), f32),
                jax.ShapeDtypeStruct((2 * size, width), f32),
            ),
            in_specs=[whole] * 4,
            out_specs=(whole, whole),
            scratch_shapes=[pltpu.VMEM((width, size), f32)],
            compiler_params=params,
            cost_estimate=cost,
            name="early",
        )(gathered, mine, lower, upper)
        n_steps = panel_index.shape[0]
        n_out = 2 if step + 1 < n_steps else 1
        block, *own = pl.pallas_call(
            functools.partial(late_kernel, n_row, step, n_steps),
            out_shape=(
                jax.ShapeDtypeStruct(matrix.shape, f32),
                jax.ShapeDtypeStruct((size, size), f32),
            )[:n_out],
            in_specs=[scalars] + [whole] * 5,
            out_specs=(whole, whole)[:n_out],
            scratch_shapes=[
                pltpu.VMEM((2 * size, width), f32),
            ],
            compiler_params=params,
            cost_estimate=cost,
            name="late",
        )(flags, other, part, rows, upper, block)
        own = own[0] if own else None
    return block


def solution(mesh):
    return jax.shard_map(
        local,
        mesh=mesh,
        in_specs=(P("row", "col"), P(None, "row"), P(None, "col"), P(), P(), P()),
        out_specs=P("row", "col"),
        check_vma=False,
    )
```

```python
import functools

import jax
import jax.numpy as jnp
from jax import lax
from jax.experimental import pallas as pl
from jax.experimental.pallas import tpu as pltpu
from jax.sharding import PartitionSpec as P

VMEM_BYTES = 20 * 1024 * 1024


def split(value):
    high = value.astype(jnp.bfloat16)
    low = (value - high.astype(jnp.float32)).astype(jnp.bfloat16)
    return high, low


def dot(a, b):
    (a_high, a_low), (b_high, b_low) = a, b
    mul = functools.partial(jnp.dot, preferred_element_type=jnp.float32)
    return mul(a_high, b_high) + (mul(a_high, b_low) + mul(a_low, b_high))


def early_kernel(n_row, gathered_ref, mine_ref, lower_ref, upper_ref, rows_out, cols_out, rows):
    size = rows.shape[1]
    piece = size // n_row
    for r in range(n_row):
        at = 2 * piece * r
        rows[piece * r : piece * (r + 1)] = gathered_ref[at : at + piece]
        rows[size + piece * r : size + piece * (r + 1)] = gathered_ref[
            at + piece : at + 2 * piece
        ]
    half = pl.ds(pl.multiple_of((lax.axis_index("col") & 1) * size, size), size)
    rows_out[...] = dot(split(lower_ref[...]), split(rows[...]))
    cols_out[...] = dot(split(mine_ref[...]), split(upper_ref[half]))


def late_kernel(
    n_row,
    step,
    n_steps,
    flags,
    other_ref,
    part_ref,
    rows_ref,
    upper_ref,
    block_ref,
    out_ref,
    *rest,
):
    own_ref, cols = rest if step + 1 < n_steps else (None, *rest)
    size = rows_ref.shape[1]
    my_row, my_col = lax.axis_index("row"), lax.axis_index("col")
    core = my_col & 1
    first = flags[6 + step]
    half = pl.ds(pl.multiple_of((1 - core) * size, size), size)
    cols[...] = part_ref[...] + dot(split(other_ref[...]), split(upper_ref[half]))
    col_hit = flags[4 + step] > 0
    rows = rows_ref[...]
    kept = split(jnp.where(col_hit, rows, jnp.float32(0.0)))
    owner = (my_col >> 1) == (first >> 1)
    next_slot = lax.div(flags[6 + (step + 1) % n_steps], n_row)
    for slot in range(2):
        at = slice(slot * size, (slot + 1) * size)
        row_hit = flags[2 * step + slot] > 0
        whole = cols[at]
        masked = jnp.where(row_hit, whole, jnp.float32(0.0))
        new = block_ref[at] - dot(split(masked), kept)
        own = jnp.where(core == 0, whole[:, :size], whole[:, size:])
        new = jnp.where(owner & row_hit, own, new)
        for member in range(2):
            here = (
                (my_row == lax.rem(first + member, n_row))
                & (slot == lax.div(first, n_row))
                & col_hit
            )
            new = jnp.where(here, rows[member * size : (member + 1) * size], new)
        out_ref[at] = new

        if own_ref is not None:

            @pl.when(next_slot == slot)
            def _():
                own_ref[...] = out_ref[at]


def local(matrix, row_struct, col_struct, panel_index, lower_inv, upper_inv):
    n_row = lax.axis_size("row")
    n_col = lax.axis_size("col")
    n_z = n_col // 2
    my_z = lax.axis_index("col") >> 1
    width = upper_inv.shape[1]
    size = width // 2
    piece = size // n_row

    def send_z(value, hops):
        pairs = [(2 * (a % n_z) + c, 2 * (b % n_z) + c) for a, b in hops for c in range(2)]
        return lax.ppermute(value, "col", pairs)

    def from_class(value, place, spacing, hop):
        return send_z(value, [(z, z + hop) for z in range(place % spacing, n_z, spacing)])

    def exchange(value):
        return lax.all_to_all(value, "row", 0, 0, tiled=True)

    def to_leaders(sends):
        def run(block, own, first):
            dist = (my_z - (first >> 1)) & (n_z - 1)
            got = [from_class(block, place, spacing, hop) for place, spacing, hop in sends]
            if own is None:
                own_at = (first >> (n_row.bit_length() - 1)) * size
                own = lax.dynamic_slice_in_dim(block, own_at.astype(jnp.uint32), size, 0)
            chunk_at = ((first & (n_row - 1)) * piece).astype(jnp.uint32)
            chunk = lax.dynamic_slice_in_dim(exchange(own), chunk_at, 2 * piece, 0)
            tiled, middle = lax.optimization_barrier((jnp.tile(chunk, (n_row, 1)), block))
            for (_, _, hop), value in zip(sends, got):
                middle = jnp.where(dist == hop % n_z, value, middle)
            return middle, tiled

        return run

    def fetch(step, block, own, later):
        first = later[3][step]
        plane = first >> 1
        which = jnp.where(
            plane & 3 == 3, 6 + (plane >> 2), (plane & 3) + 3 * ((plane >> 2) & 1)
        )
        middle, tiled = lax.switch(which, leads, block, own, first)
        tiled, later = lax.optimization_barrier((tiled, later))
        later = later[0][step], later[1][step], later[2], later[3]
        halves = lax.optimization_barrier((middle[:size], middle[size:], tiled))
        up = from_class(middle, 3, 4, 1)
        down = from_class(middle, 3, 4, -1)
        top = from_class(halves[0], 3, 4, 2)
        bottom = from_class(halves[1], 3, 4, -2)
        gathered = exchange(halves[2])
        near = my_z & 3
        up, later = lax.optimization_barrier((up, later))
        both = jnp.concatenate([top, bottom], axis=0)
        columns = jnp.where(
            near == 3, middle, jnp.where(near == 0, up, jnp.where(near == 2, down, both))
        )
        return columns, gathered, later

    leads = []
    for place in (0, 1, 2, 4, 5, 6):
        hops = [hop - place % 4 for hop in (7, -5, 3, -1)]
        hops.sort(key=abs)
        leads.append(to_leaders([(place, 8 if abs(hop) > 3 else 4, hop) for hop in hops]))
    for place in range(3, n_z, 4):
        leads.append(to_leaders([(place, n_z, hop) for hop in (-4, 4, 8)]))
    whole = pl.BlockSpec(memory_space=pltpu.VMEM)
    scalars = pl.BlockSpec(memory_space=pltpu.SMEM)
    params = pltpu.CompilerParams(vmem_limit_bytes=VMEM_BYTES)
    cost = pl.CostEstimate(
        flops=6 * width * width * width, bytes_accessed=12 * width * width, transcendentals=0
    )
    f32 = jnp.float32
    flags = jnp.concatenate([row_struct.reshape(-1), col_struct.reshape(-1), panel_index])

    block, own, panels = matrix, None, panel_index
    for step in range(panel_index.shape[0]):
        later = lower_inv, upper_inv, flags, panels
        mine, gathered, (lower, upper, flags, panels) = fetch(step, block, own, later)
        other = lax.ppermute(mine, "col", [(i, i ^ 1) for i in range(n_col)])
        rows, part = pl.pallas_call(
            functools.partial(early_kernel, n_row),
            out_shape=(
                jax.ShapeDtypeStruct((width, size), f32),
                jax.ShapeDtypeStruct((2 * size, width), f32),
            ),
            in_specs=[whole] * 4,
            out_specs=(whole, whole),
            scratch_shapes=[pltpu.VMEM((width, size), f32)],
            compiler_params=params,
            cost_estimate=cost,
            name="early",
        )(gathered, mine, lower, upper)
        n_steps = panel_index.shape[0]
        n_out = 2 if step + 1 < n_steps else 1
        block, *own = pl.pallas_call(
            functools.partial(late_kernel, n_row, step, n_steps),
            out_shape=(
                jax.ShapeDtypeStruct(matrix.shape, f32),
                jax.ShapeDtypeStruct((size, size), f32),
            )[:n_out],
            in_specs=[scalars] + [whole] * 5,
            out_specs=(whole, whole)[:n_out],
            scratch_shapes=[
                pltpu.VMEM((2 * size, width), f32),
            ],
            compiler_params=params,
            cost_estimate=cost,
            name="late",
        )(flags, other, part, rows, upper, block)
        own = own[0] if own else None
    return block


def solution(mesh):
    return jax.shard_map(
        local,
        mesh=mesh,
        in_specs=(P("row", "col"), P(None, "row"), P(None, "col"), P(), P(), P()),
        out_specs=P("row", "col"),
        check_vma=False,
    )
```

```python
import functools

import jax
import jax.numpy as jnp
from jax import lax
from jax.experimental import pallas as pl
from jax.experimental.pallas import tpu as pltpu
from jax.sharding import PartitionSpec as P

VMEM_BYTES = 20 * 1024 * 1024


def split(value):
    high = value.astype(jnp.bfloat16)
    low = (value - high.astype(jnp.float32)).astype(jnp.bfloat16)
    return high, low


def dot(a, b):
    (a_high, a_low), (b_high, b_low) = a, b
    mul = functools.partial(jnp.dot, preferred_element_type=jnp.float32)
    return mul(a_high, b_high) + (mul(a_high, b_low) + mul(a_low, b_high))


def early_kernel(n_row, gathered_ref, mine_ref, lower_ref, upper_ref, rows_out, cols_out, rows):
    size = rows.shape[1]
    piece = size // n_row
    for r in range(n_row):
        at = 2 * piece * r
        rows[piece * r : piece * (r + 1)] = gathered_ref[at : at + piece]
        rows[size + piece * r : size + piece * (r + 1)] = gathered_ref[
            at + piece : at + 2 * piece
        ]
    half = pl.ds(pl.multiple_of((lax.axis_index("col") & 1) * size, size), size)
    rows_out[...] = dot(split(lower_ref[...]), split(rows[...]))
    cols_out[...] = dot(split(mine_ref[...]), split(upper_ref[half]))


def late_kernel(
    n_row,
    step,
    n_steps,
    flags,
    other_ref,
    part_ref,
    rows_ref,
    upper_ref,
    block_ref,
    out_ref,
    *rest,
):
    own_ref, cols = rest if step + 1 < n_steps else (None, *rest)
    size = rows_ref.shape[1]
    my_row, my_col = lax.axis_index("row"), lax.axis_index("col")
    core = my_col & 1
    first = flags[6 + step]
    half = pl.ds(pl.multiple_of((1 - core) * size, size), size)
    cols[...] = part_ref[...] + dot(split(other_ref[...]), split(upper_ref[half]))
    col_hit = flags[4 + step] > 0
    rows = rows_ref[...]
    kept = split(jnp.where(col_hit, rows, jnp.float32(0.0)))
    owner = (my_col >> 1) == (first >> 1)
    next_slot = lax.div(flags[6 + (step + 1) % n_steps], n_row)
    for slot in range(2):
        at = slice(slot * size, (slot + 1) * size)
        row_hit = flags[2 * step + slot] > 0
        whole = cols[at]
        masked = jnp.where(row_hit, whole, jnp.float32(0.0))
        new = block_ref[at] - dot(split(masked), kept)
        own = jnp.where(core == 0, whole[:, :size], whole[:, size:])
        new = jnp.where(owner & row_hit, own, new)
        for member in range(2):
            here = (
                (my_row == lax.rem(first + member, n_row))
                & (slot == lax.div(first, n_row))
                & col_hit
            )
            new = jnp.where(here, rows[member * size : (member + 1) * size], new)
        out_ref[at] = new

        if own_ref is not None:

            @pl.when(next_slot == slot)
            def _():
                own_ref[...] = out_ref[at]


def local(matrix, row_struct, col_struct, panel_index, lower_inv, upper_inv):
    n_row = lax.axis_size("row")
    n_col = lax.axis_size("col")
    n_z = n_col // 2
    my_z = lax.axis_index("col") >> 1
    width = upper_inv.shape[1]
    size = width // 2
    piece = size // n_row

    def send_z(value, hops):
        pairs = [(2 * (a % n_z) + c, 2 * (b % n_z) + c) for a, b in hops for c in range(2)]
        return lax.ppermute(value, "col", pairs)

    def from_class(value, place, spacing, hop):
        return send_z(value, [(z, z + hop) for z in range(place % spacing, n_z, spacing)])

    def exchange(value):
        return lax.all_to_all(value, "row", 0, 0, tiled=True)

    def to_leaders(sends):
        def run(block, own, first):
            dist = (my_z - (first >> 1)) & (n_z - 1)
            got = [from_class(block, place, spacing, hop) for place, spacing, hop in sends]
            if own is None:
                own_at = (first >> (n_row.bit_length() - 1)) * size
                own = lax.dynamic_slice_in_dim(block, own_at.astype(jnp.uint32), size, 0)
            chunk_at = ((first & (n_row - 1)) * piece).astype(jnp.uint32)
            chunk = lax.dynamic_slice_in_dim(exchange(own), chunk_at, 2 * piece, 0)
            chunk, middle = lax.optimization_barrier((chunk, block))
            for (_, _, hop), value in zip(sends, got):
                middle = jnp.where(dist == hop % n_z, value, middle)
            return middle, chunk

        return run

    def fetch(step, block, own, later):
        first = later[3][step]
        plane = first >> 1
        which = jnp.where(
            plane & 3 == 3, 6 + (plane >> 2), (plane & 3) + 3 * ((plane >> 2) & 1)
        )
        middle, chunk = lax.switch(which, leads, block, own, first)
        chunk, later = lax.optimization_barrier((chunk, later))
        later = later[0][step], later[1][step], later[2], later[3]
        up = from_class(middle, 3, 4, 1)
        down = from_class(middle, 3, 4, -1)
        top = from_class(middle[:size], 3, 4, 2)
        bottom = from_class(middle[size:], 3, 4, -2)
        gathered = exchange(jnp.tile(chunk, (n_row, 1)))
        near = my_z & 3
        up, later = lax.optimization_barrier((up, later))
        both = jnp.concatenate([top, bottom], axis=0)
        columns = jnp.where(
            near == 3, middle, jnp.where(near == 0, up, jnp.where(near == 2, down, both))
        )
        return columns, gathered, later

    leads = []
    for place in (0, 1, 2, 4, 5, 6):
        hops = [hop - place % 4 for hop in (7, -5, 3, -1)]
        hops.sort(key=abs)
        leads.append(to_leaders([(place, 8 if abs(hop) > 3 else 4, hop) for hop in hops]))
    for place in range(3, n_z, 4):
        leads.append(to_leaders([(place, n_z, hop) for hop in (-4, 4, 8)]))
    whole = pl.BlockSpec(memory_space=pltpu.VMEM)
    scalars = pl.BlockSpec(memory_space=pltpu.SMEM)
    params = pltpu.CompilerParams(vmem_limit_bytes=VMEM_BYTES)
    cost = pl.CostEstimate(
        flops=6 * width * width * width, bytes_accessed=12 * width * width, transcendentals=0
    )
    f32 = jnp.float32
    flags = jnp.concatenate([row_struct.reshape(-1), col_struct.reshape(-1), panel_index])

    block, own, panels = matrix, None, panel_index
    for step in range(panel_index.shape[0]):
        later = lower_inv, upper_inv, flags, panels
        mine, gathered, (lower, upper, flags, panels) = fetch(step, block, own, later)
        other = lax.ppermute(mine, "col", [(i, i ^ 1) for i in range(n_col)])
        rows, part = pl.pallas_call(
            functools.partial(early_kernel, n_row),
            out_shape=(
                jax.ShapeDtypeStruct((width, size), f32),
                jax.ShapeDtypeStruct((2 * size, width), f32),
            ),
            in_specs=[whole] * 4,
            out_specs=(whole, whole),
            scratch_shapes=[pltpu.VMEM((width, size), f32)],
            compiler_params=params,
            cost_estimate=cost,
            name="early",
        )(gathered, mine, lower, upper)
        n_steps = panel_index.shape[0]
        n_out = 2 if step + 1 < n_steps else 1
        block, *own = pl.pallas_call(
            functools.partial(late_kernel, n_row, step, n_steps),
            out_shape=(
                jax.ShapeDtypeStruct(matrix.shape, f32),
                jax.ShapeDtypeStruct((size, size), f32),
            )[:n_out],
            in_specs=[scalars] + [whole] * 5,
            out_specs=(whole, whole)[:n_out],
            scratch_shapes=[
                pltpu.VMEM((2 * size, width), f32),
            ],
            compiler_params=params,
            cost_estimate=cost,
            name="late",
        )(flags, other, part, rows, upper, block)
        own = own[0] if own else None
    return block


def solution(mesh):
    return jax.shard_map(
        local,
        mesh=mesh,
        in_specs=(P("row", "col"), P(None, "row"), P(None, "col"), P(), P(), P()),
        out_specs=P("row", "col"),
        check_vma=False,
    )
```
